512 devices in a mesh: brick: 32 (over z, x), group: 16 (over y, core).
Axes of the slice: x: 4, y: 8, z: 8, core: 2. Of those that a mesh axis runs over, the one named last changes fastest.
Arguments:
- right_side: float32 [512, 256, 128], P('brick', 'group'), may hold values from -8 to 8
- mass_coef: float32 [512, 256, 128], P('brick', 'group'), may hold values from 0.25 to 4
- face_coef: float32 [512, 256, 128], P('brick', 'group'), may hold values from 0.25 to 4
Outputs:
- fine_fix: float32 [512, 256, 128], P('brick', 'group')
- middle_fix: float32 [256, 128, 64], P('brick', 'group')
- coarse_fix: float32 [128, 64, 32], P('brick', 'group')
- coarse_rhs: float32 [64, 32, 16], P('brick')
The draws below stay inside these ranges and needn't reach their ends.
All inputs are finite; a program needn't handle non-finite values.
Results may differ from the reference program's by a relative error of at most 0.00019.
Values sent between devices are 32-bit elements; how exact they have to be, the bound alone decides.
A program may use at most 64 MiB of HBM per device.

```python
import math
import jax
import jax.numpy as jnp

LEVELS = 3
NX = 512
NY = 256
NZ = 128


def level_of(own_key, extent, shards, least, high):
    level = 1.0
    for dim, parts in shards:
        steps = jax.random.uniform(jax.random.fold_in(jax.random.fold_in(own_key, 6), dim), (parts,), jnp.float32, least / len(shards), high / len(shards))
        level = level * jnp.repeat(jnp.exp(steps), extent[dim] // parts).reshape((-1,) + (1,) * (len(extent) - 1 - dim))
    return level


def centred(rng, extent, scale, reach, shards=(), held_as=jnp.bfloat16):
    values = scale * jax.random.normal(rng, extent, jnp.float32)
    if shards:
        values = values * level_of(rng, extent, shards, -0.22, 0.18)
    return jnp.clip(values, -reach, reach).astype(held_as)


def setup_inputs(seed: int = 0) -> dict:
    arg_keys = jax.random.split(jax.random.key(seed), 4)
    right_side = centred(arg_keys[0], (NX, NY, NZ), 1.0, 8.0, ((0, 32), (1, 16)), jnp.float32)
    mass_coef = jnp.clip(jnp.exp(math.log(4.0) - 2.7725887 * jax.random.uniform(arg_keys[1], (NX, NY, NZ), jnp.float32) ** level_of(arg_keys[1], (NX, NY, NZ), ((0, 32), (1, 16)), -0.2, 0.2)), 0.25, 4.0)
    face_coef = jnp.clip(jnp.exp(math.log(4.0) - 2.7725887 * jax.random.uniform(arg_keys[2], (NX, NY, NZ), jnp.float32) ** level_of(arg_keys[2], (NX, NY, NZ), ((0, 32), (1, 16)), -0.2, 0.2)), 0.25, 4.0)
    return dict(right_side=right_side, mass_coef=mass_coef, face_coef=face_coef)


stencil_weight = 0.25
center_value = 1.1
half_width = 0.8
ratio_sigma = center_value / half_width
first_rho = 1.0 / ratio_sigma
second_rho = 1.0 / (2.0 * ratio_sigma - first_rho)
carry_factor = second_rho * first_rho
push_factor = 2.0 * second_rho / half_width


def interior(field):
    return field[1:-1, 1:-1, :]


def neighbours(field):
    padded = jnp.pad(field, ((0, 0), (0, 0), (1, 1)))
    return [field[2:, 1:-1, :], field[:-2, 1:-1, :], field[1:-1, 2:, :], field[1:-1, :-2, :],
            padded[1:-1, 1:-1, 2:], padded[1:-1, 1:-1, :-2]]


def face_weights(face_coef):
    center = interior(face_coef)
    return [stencil_weight * 0.5 * (center + beside) for beside in neighbours(face_coef)]


def operate(field, mass_inner, weights_list):
    center = interior(field)
    total = mass_inner * center
    for weight_term, beside in zip(weights_list, neighbours(field)):
        total = total + weight_term * (center - beside)
    return total


def diagonal_of(mass_inner, weights_list):
    total = mass_inner
    for weight_term in weights_list:
        total = total + weight_term
    return total


def loop_pad(field):
    return jnp.pad(field, ((1, 1), (1, 1), (0, 0)))


def restrict(field):
    shaped = field.reshape(field.shape[0] // 2, 2, field.shape[1] // 2, 2, field.shape[2] // 2, 2)
    return shaped.mean(axis=(1, 3, 5))


def smooth_level(source, mass_coef, face_coef):
    weights_list = face_weights(loop_pad(face_coef))
    diagonal = diagonal_of(mass_coef, weights_list)
    first_step = source / diagonal / center_value
    first_resid = source - operate(loop_pad(first_step), mass_coef, weights_list)
    second_iter = first_step + carry_factor * first_step + push_factor * first_resid / diagonal
    residual = source - operate(loop_pad(second_iter), mass_coef, weights_list)
    return second_iter, residual


def reference(right_side, mass_coef, face_coef):
    source = right_side
    corrections = []
    for tier_index in range(LEVELS):
        correction, residual = smooth_level(source, mass_coef, face_coef)
        corrections.append(correction)
        source = restrict(residual)
        mass_coef = restrict(mass_coef)
        face_coef = restrict(face_coef)
    return corrections[0], corrections[1], corrections[2], source
```

```python
import functools

import jax
import jax.numpy as jnp
from jax import lax
from jax.experimental import pallas as pl
from jax.experimental.pallas import tpu as pltpu
from jax.sharding import PartitionSpec as P

MESH = pl.DeviceIdType.MESH

center_value = 1.1
half_width = 0.8
ratio_sigma = center_value / half_width
first_rho = 1.0 / ratio_sigma
second_rho = 1.0 / (2.0 * ratio_sigma - first_rho)
carry_factor = second_rho * first_rho
push_factor = 2.0 * second_rho / half_width

alpha = (1.0 + carry_factor) / center_value + push_factor * (1.0 - 1.0 / center_value)
beta = push_factor / center_value

OUTSIDE_MASS = 1e30
LANES = 128
I0, J0, W0, E0 = 3, 8, 16, (22, 32, LANES)
I1, W1, E1 = 8, 8, (24, 24, LANES)

DIRS = [(1, 0), (-1, 0), (1, 1), (1, -1), (-1, 1), (-1, -1), (0, 1), (0, -1)]


def cut(step, start, size, width):
    if step == 0:
        return start, start, size
    if step > 0:
        return start + size - width, start - width, width
    return start, start + size, width


def lane_shift(a, by, lane):
    low = jnp.where(lane >= by, pltpu.roll(a, by, axis=2), 0.0)
    high = jnp.where(lane < LANES - by, pltpu.roll(a, LANES - by, axis=2), 0.0)
    return low + high


def around(a, by):
    mid = a[1:-1]
    cols = a.shape[1]
    lane = lax.broadcasted_iota(jnp.int32, mid.shape, 2)
    total = a[2:] + a[:-2]
    total = total + pltpu.roll(mid, 1, axis=1) + pltpu.roll(mid, cols - 1, axis=1)
    return total + lane_shift(mid, by, lane)


def spread(u, c, by):
    return c[1:-1] * around(u, by) + around(c * u, by)


def inverse(m, c, by):
    diag = m[1:-1] + 6.0 * c[1:-1] + around(c, by)
    rough = pl.reciprocal(diag, approx=True)
    rough = rough * (2.0 - diag * rough)
    return rough * (2.0 - diag * rough)


def smooth(f, c, invd, by):
    s = beta * spread(f * invd, c, by)
    x2 = invd[1:-1] * (alpha * f[1:-1] + s)
    r2 = (1.0 - alpha) * f[2:-2] - s[1:-1] + spread(x2, c[1:-1], by)
    return x2, r2


def pool(a, scratch, by):
    rows, cols, _ = a.shape
    pair = a.reshape(rows // 2, 2, cols, LANES)
    scratch[0 : rows // 2, 0:cols, :] = pair[:, 0] + pair[:, 1]
    even = scratch[0 : rows // 2, pl.ds(0, cols // 2, stride=2), :]
    odd = scratch[0 : rows // 2, pl.ds(1, cols // 2, stride=2), :]
    both = even + odd
    return 0.125 * (both + pltpu.roll(both, LANES - by, axis=2))


def squeeze(a, by):
    shape = (LANES, LANES // by)
    pick = lax.broadcasted_iota(jnp.int32, shape, 0) == by * lax.broadcasted_iota(jnp.int32, shape, 1)
    return lax.dot(
        a, pick.astype(jnp.float32), precision=lax.Precision.HIGHEST, preferred_element_type=jnp.float32
    )


def main_kernel(
    bricks, groups,
    f_ref, m_ref, c_ref,
    fine_ref, middle_ref, coarse_ref, gather_ref,
    x0, x1, f1, pool0, pool1, pool2, f3,
    fine_buf, middle_buf, coarse_buf,
    load_sem, out_sem, send_a, recv_a, send_b, recv_b, send_c, recv_c, send_d, recv_d,
):
    b, g = lax.axis_index("brick"), lax.axis_index("group")

    loads = [
        pltpu.make_async_copy(ref, x0.at[i, pl.ds(I0, W0), pl.ds(J0, W0), :], load_sem.at[i])
        for i, ref in enumerate((f_ref, m_ref, c_ref))
    ]
    for copy in loads:
        copy.start()

    barrier = pltpu.get_barrier_semaphore()

    def reach(step):
        db, dg = step
        ok = (b + db >= 0) & (b + db < bricks) & (g + dg >= 0) & (g + dg < groups)
        return ok, {"brick": b + db, "group": g + dg}

    expected = groups - 1
    for step in DIRS[:6]:
        ok, peer = reach(step)
        expected = expected + ok.astype(jnp.int32)

        @pl.when(ok)
        def _():
            pl.semaphore_signal(barrier, inc=1, device_id=peer, device_id_type=MESH)

    def mate(k):
        return {"brick": b, "group": lax.rem(g + k, groups)}

    for k in range(1, groups):
        pl.semaphore_signal(barrier, inc=1, device_id=mate(k), device_id_type=MESH)

    def blank(rows0, cols0, rows1, cols1):
        for ref, rows, cols in ((x0, rows0, cols0), (x1, rows1, cols1)):
            shape = (rows.size, cols.size, LANES)
            if ref is x0:
                ref[0, rows, cols, :] = jnp.zeros(shape, jnp.float32)
                ref[1, rows, cols, :] = jnp.full(shape, OUTSIDE_MASS, jnp.float32)
                ref[2, rows, cols, :] = jnp.zeros(shape, jnp.float32)
            else:
                ref[0, rows, cols, :] = jnp.full(shape, OUTSIDE_MASS, jnp.float32)
                ref[1, rows, cols, :] = jnp.zeros(shape, jnp.float32)
                f1[rows, cols, :] = jnp.zeros(shape, jnp.float32)

    every0, every1 = pl.ds(0, E0[1]), pl.ds(0, E1[1])

    @pl.when(b == 0)
    def _():
        blank(pl.ds(0, I0), every0, pl.ds(0, I1), every1)

    @pl.when(b == bricks - 1)
    def _():
        blank(pl.ds(I0 + W0, I0), every0, pl.ds(I1 + W1, I1), every1)

    @pl.when(g == 0)
    def _():
        blank(pl.ds(0, E0[0]), pl.ds(0, J0), pl.ds(0, E1[0]), pl.ds(0, I1))

    @pl.when(g == groups - 1)
    def _():
        blank(pl.ds(0, E0[0]), pl.ds(J0 + W0, J0), pl.ds(0, E1[0]), pl.ds(I1 + W1, I1))

    for copy in loads:
        copy.wait()
    own0 = (pl.ds(I0, W0), pl.ds(J0, W0))
    own1 = (pl.ds(I1, W1), pl.ds(I1, W1))
    x1[(0, *own1)] = pool(x0[(1, *own0)], pool0, 1)
    x1[(1, *own1)] = pool(x0[(2, *own0)], pool0, 1)

    pl.semaphore_wait(barrier, expected)

    def message(ref, lead, step, widths, at, sizes, send, recv, peer):
        si, ti, ni = cut(step[0], at[0], sizes[0], widths[0])
        sj, tj, nj = cut(step[1], at[1], sizes[1], widths[1])
        return pltpu.make_async_remote_copy(
            src_ref=ref.at[(*lead, pl.ds(si, ni), pl.ds(sj, nj))],
            dst_ref=ref.at[(*lead, pl.ds(ti, ni), pl.ds(tj, nj))],
            send_sem=send, recv_sem=recv, device_id=peer, device_id_type=MESH,
        )

    def stage_a(i, step, peer):
        at, sizes = (I0, J0), (W0, W0)
        if step[0] and step[1]:
            return [message(x0, (pl.ds(0, 3),), step, (2, 2), at, sizes, send_a.at[i, 0], recv_a.at[i, 0], peer)]
        return [
            message(x0, (pl.ds(0, 2),), step, (2, 2), at, sizes, send_a.at[i, 0], recv_a.at[i, 0], peer),
            message(x0, (2,), step, (3, 3), at, sizes, send_a.at[i, 1], recv_a.at[i, 1], peer),
        ]

    def stage_b(i, step, peer):
        rows = 6 if step[1] else 7
        return [message(x1, (pl.ds(0, 2),), step, (rows, W1), (I1, I1), (W1, W1), send_b.at[i], recv_b.at[i], peer)]

    def stage_c(i, step, peer):
        rows = 5 if step[1] else 6
        return [message(f1, (), step, (rows, W1), (I1, I1), (W1, W1), send_c.at[i], recv_c.at[i], peer)]

    def each(stage, act):
        for i, step in enumerate(DIRS):
            ok, peer = reach(step)

            @pl.when(ok)
            def _():
                for copy in stage(i, step, peer):
                    act(copy)

    def receive(stage):
        for i, step in enumerate(DIRS):
            ok, peer = reach((-step[0], -step[1]))

            @pl.when(ok)
            def _():
                for copy in stage(i, step, peer):
                    copy.wait_recv()

    each(stage_a, lambda copy: copy.start())
    each(stage_b, lambda copy: copy.start())

    receive(stage_a)
    f, m, c = x0[0], x0[1], 0.125 * x0[2]
    invd = inverse(m, c, 1)
    x2, r2 = smooth(f[1:-1], c[1:-1], invd, 1)
    fine_buf[...] = x2[1:-1, J0 : J0 + W0]
    f1[own1] = pool(r2[:, J0 : J0 + W0], pool0, 1)
    each(stage_c, lambda copy: copy.start())
    fine_out = pltpu.make_async_copy(fine_buf, fine_ref, out_sem.at[0])
    fine_out.start()

    receive(stage_b)
    m1, c1 = x1[0], x1[1]
    c2 = 0.125 * pool(c1, pool1, 2)
    m2 = pool(m1, pool1, 2)
    c1 = 0.125 * c1
    invd1 = inverse(m1, c1, 2)
    invd2 = inverse(m2, c2, 4)

    receive(stage_c)
    x2, r2 = smooth(f1[2:22], c1[2:22], invd1[1:21], 2)
    middle = x2[5:13, I1 : I1 + W1]
    f2 = pool(r2, pool1, 2)
    x2, r2 = smooth(f2, c2[2:10], invd2[1:9], 4)
    coarse = x2[1:5, 4:8]
    pool2[...] = jnp.stack([r2[0] + r2[1], r2[2] + r2[3]])
    both = pool2[:, pl.ds(4, 2, stride=2), :] + pool2[:, pl.ds(5, 2, stride=2), :]
    f3[...] = 0.125 * (both + pltpu.roll(both, LANES - 4, axis=2))

    keep = pltpu.make_async_copy(f3, gather_ref.at[:, g], out_sem.at[1])
    keep.start()

    def share(k):
        return pltpu.make_async_remote_copy(
            src_ref=f3, dst_ref=gather_ref.at[:, g], send_sem=send_d.at[k], recv_sem=recv_d.at[k],
            device_id=mate(k), device_id_type=MESH,
        )

    def shared(k):
        owner = lax.rem(g + groups - k, groups)
        return pltpu.make_async_remote_copy(
            src_ref=f3, dst_ref=gather_ref.at[:, owner], send_sem=send_d.at[k], recv_sem=recv_d.at[k],
            device_id=mate(k), device_id_type=MESH,
        )

    for k in range(1, groups):
        share(k).start()

    middle_buf[...] = squeeze(middle.reshape(W1 * W1, LANES), 2).reshape(W1, W1, LANES // 2)
    for i in range(4):
        coarse_buf[i] = squeeze(coarse[i], 4)
    outs = [
        pltpu.make_async_copy(middle_buf, middle_ref, out_sem.at[2]),
        pltpu.make_async_copy(coarse_buf, coarse_ref, out_sem.at[3]),
    ]
    for copy in outs:
        copy.start()

    for k in range(1, groups):
        shared(k).wait_recv()
    for copy in (fine_out, keep, *outs):
        copy.wait()
    each(stage_a, lambda copy: copy.wait_send())
    each(stage_b, lambda copy: copy.wait_send())
    each(stage_c, lambda copy: copy.wait_send())
    for k in range(1, groups):
        share(k).wait_send()


def finish_kernel(fine, middle, coarse, gathered, fine_out, middle_out, coarse_out, rhs_out):
    fine_out[...] = fine[...]
    middle_out[...] = middle[...]
    coarse_out[...] = coarse[...]
    depth = rhs_out.shape[1]
    shape = (depth, LANES)
    pick = 8 * lax.broadcasted_iota(jnp.int32, shape, 0) == lax.broadcasted_iota(jnp.int32, shape, 1)
    for i in range(2):
        rhs_out[i] = lax.dot_general(
            pick.astype(jnp.float32), gathered[i], (((1,), (1,)), ((), ())),
            precision=lax.Precision.HIGHEST, preferred_element_type=jnp.float32,
        )


def solution(mesh):
    bricks, groups = mesh.shape["brick"], mesh.shape["group"]
    anywhere = pl.BlockSpec(memory_space=pl.ANY)
    vmem = pl.BlockSpec(memory_space=pltpu.VMEM)

    def f32(*shape):
        return jax.ShapeDtypeStruct(shape, jnp.float32)

    def buf(*shape):
        return pltpu.VMEM(shape, jnp.float32)

    dma = pltpu.SemaphoreType.DMA

    def body(right_side, mass_coef, face_coef):
        small = (f32(W0, W0, LANES), f32(W1, W1, LANES // 2), f32(4, 4, LANES // 4))
        fine, middle, coarse, gathered = pl.pallas_call(
            functools.partial(main_kernel, bricks, groups),
            out_shape=(*small, f32(2, groups, 2, LANES)),
            in_specs=[anywhere] * 3,
            out_specs=(anywhere,) * 4,
            scratch_shapes=[
                buf(3, *E0), buf(2, *E1), buf(*E1),
                buf(8, 16, LANES), buf(12, 24, LANES), buf(2, 12, LANES), buf(2, 2, LANES),
                buf(W0, W0, LANES), buf(W1, W1, LANES // 2), buf(4, 4, LANES // 4),
                dma((3,)), dma((4,)), dma((8, 2)), dma((8, 2)), dma((8,)), dma((8,)), dma((8,)), dma((8,)),
                dma((groups,)), dma((groups,)),
            ],
            compiler_params=pltpu.CompilerParams(
                collective_id=0, has_side_effects=True, vmem_limit_bytes=32 * 1024 * 1024
            ),
            name="cycle",
        )(right_side, mass_coef, face_coef)
        fine, middle, coarse, rhs = pl.pallas_call(
            finish_kernel,
            out_shape=(*small, f32(2, LANES // 8, 2 * groups)),
            in_specs=[vmem] * 4,
            out_specs=(vmem,) * 4,
            name="finish",
        )(fine, middle, coarse, gathered.reshape(2, 2 * groups, LANES))
        return fine, middle, coarse, jnp.swapaxes(rhs, 1, 2)

    placed = P("brick", "group", None)
    return jax.shard_map(
        body,
        mesh=mesh,
        in_specs=(placed, placed, placed),
        out_specs=(placed, placed, placed, P("brick", None, None)),
        check_vma=False,
    )
```

```python
import functools

import jax
import jax.numpy as jnp
from jax import lax
from jax.experimental import pallas as pl
from jax.experimental.pallas import tpu as pltpu
from jax.sharding import PartitionSpec as P

MESH = pl.DeviceIdType.MESH

center_value = 1.1
half_width = 0.8
ratio_sigma = center_value / half_width
first_rho = 1.0 / ratio_sigma
second_rho = 1.0 / (2.0 * ratio_sigma - first_rho)
carry_factor = second_rho * first_rho
push_factor = 2.0 * second_rho / half_width

alpha = (1.0 + carry_factor) / center_value + push_factor * (1.0 - 1.0 / center_value)
beta = push_factor / center_value

OUTSIDE_MASS = 1e30
LANES = 128
I0, J0, W0, E0 = 3, 8, 16, (22, 32, LANES)
I1, H1, J1, W1, E1 = 4, 4, 8, 8, (12, 24, LANES)

DIRS = [(1, 0), (-1, 0), (1, 1), (1, -1), (-1, 1), (-1, -1), (0, 1), (0, -1)]


def cut(step, start, size, width):
    if step == 0:
        return start, start, size
    if step > 0:
        return start + size - width, start - width, width
    return start, start + size, width


def lanes_of(a):
    return lax.broadcasted_iota(jnp.int32, a.shape, a.ndim - 1)


def turn(a, by):
    return pltpu.roll(a, by % LANES, axis=a.ndim - 1)


def beside(mid, by):
    lane = lanes_of(mid)
    low = jnp.where(lane >= by, turn(mid, by), 0.0)
    high = jnp.where(lane < LANES - by, turn(mid, -by), 0.0)
    cols = mid.shape[1]
    return low + high + pltpu.roll(mid, 1, axis=1) + pltpu.roll(mid, cols - 1, axis=1)


def around(a, by):
    return a[2:] + a[:-2] + beside(a[1:-1], by)


def around_pairs(a, by):
    up, down = turn(a[:-1], -1), turn(a[1:], 1)
    even = lanes_of(a[1:-1]) % 2 == 0
    return jnp.where(even, up[1:] + up[:-1], down[1:] + down[:-1]) + beside(a[1:-1], by)


def inverse(m, c, total):
    diag = m + 0.75 * c + 0.125 * total
    rough = pl.reciprocal(diag, approx=True)
    rough = rough * (2.0 - diag * rough)
    return rough * (2.0 - diag * rough)


def squeeze(a, by, first=0):
    shape = (LANES, LANES // by)
    pick = lax.broadcasted_iota(jnp.int32, shape, 0) == by * lax.broadcasted_iota(jnp.int32, shape, 1) + first
    return lax.dot(
        a, pick.astype(jnp.float32), precision=lax.Precision.HIGHEST, preferred_element_type=jnp.float32
    )


def halve(a, scratch):
    rows, cols, _ = a.shape
    scratch[0:rows, 0:cols, :] = a
    return scratch[0:rows, pl.ds(0, cols // 2, stride=2), :] + scratch[0:rows, pl.ds(1, cols // 2, stride=2), :]


def pack_pool(a, scratch):
    rows, cols, _ = a.shape
    quad = a.reshape(rows // 4, 4, cols, LANES)
    upper, lower = halve(quad[:, 0] + quad[:, 1], scratch.at[0]), halve(quad[:, 2] + quad[:, 3], scratch.at[1])
    even = lanes_of(upper) % 2 == 0
    return 0.125 * jnp.where(even, upper + turn(upper, -1), lower + turn(lower, 1))


def unpack_pool(a, scratch):
    both = halve(a, scratch)
    both = both + turn(both, -1)
    return 0.125 * (both + turn(both, -2))


def main_kernel(
    bricks, groups,
    f_ref, m_ref, c_ref,
    fine_ref, middle_ref, coarse_ref, gather_ref,
    x0, x1, f1, inv0, y0, cy0, x20, cx20, base0, r0, pool0, pool1, pool2, f3,
    load_sem, send_a, recv_a, send_b, recv_b, send_c, recv_c, send_d, recv_d,
):
    b, g = lax.axis_index("brick"), lax.axis_index("group")
    barrier = pltpu.get_barrier_semaphore()

    def reach(step):
        db, dg = step
        ok = (b + db >= 0) & (b + db < bricks) & (g + dg >= 0) & (g + dg < groups)
        return ok, {"brick": b + db, "group": g + dg}

    def mate(k):
        return {"brick": b, "group": lax.rem(g + k, groups)}

    mates = sorted(range(1, groups), key=lambda k: (abs(2 * k - groups), k))

    expected = groups - 1
    for step in DIRS[:6]:
        ok, peer = reach(step)
        expected = expected + ok.astype(jnp.int32)

        @pl.when(ok)
        def _():
            pl.semaphore_signal(barrier, inc=1, device_id=peer, device_id_type=MESH)

    for k in mates:
        pl.semaphore_signal(barrier, inc=1, device_id=mate(k), device_id_type=MESH)

    loads = [
        pltpu.make_async_copy(ref, x0.at[i, pl.ds(I0, W0), pl.ds(J0, W0), :], load_sem.at[i])
        for i, ref in enumerate((f_ref, m_ref, c_ref))
    ]
    for copy in loads:
        copy.start()

    def blank(rows0, cols0, rows1, cols1):
        shape0, shape1 = (rows0.size, cols0.size, LANES), (rows1.size, cols1.size, LANES)
        for i, value in enumerate((0.0, OUTSIDE_MASS, 0.0)):
            x0[i, rows0, cols0, :] = jnp.full(shape0, value, jnp.float32)
        for i, value in enumerate((OUTSIDE_MASS, 0.0)):
            x1[i, rows1, cols1, :] = jnp.full(shape1, value, jnp.float32)
        f1[rows1, cols1, :] = jnp.zeros(shape1, jnp.float32)

    every = (pl.ds(0, E0[0]), pl.ds(0, E0[1]), pl.ds(0, E1[0]), pl.ds(0, E1[1]))

    @pl.when(b == 0)
    def _():
        blank(pl.ds(0, I0), every[1], pl.ds(0, I1), every[3])

    @pl.when(b == bricks - 1)
    def _():
        blank(pl.ds(I0 + W0, I0), every[1], pl.ds(I1 + H1, I1), every[3])

    @pl.when(g == 0)
    def _():
        blank(every[0], pl.ds(0, J0), every[2], pl.ds(0, J1))

    @pl.when(g == groups - 1)
    def _():
        blank(every[0], pl.ds(J0 + W0, J0), every[2], pl.ds(J1 + W1, J1))

    for copy in loads:
        copy.wait()
    own0 = (pl.ds(I0, W0), pl.ds(J0, W0))
    own1 = (pl.ds(I1, H1), pl.ds(J1, W1))
    x1[(0, *own1)] = pack_pool(x0[(1, *own0)], pool0)
    x1[(1, *own1)] = pack_pool(x0[(2, *own0)], pool0)

    pl.semaphore_wait(barrier, expected)

    def message(ref, lead, step, widths, at, sizes, send, recv, peer):
        si, ti, ni = cut(step[0], at[0], sizes[0], widths[0])
        sj, tj, nj = cut(step[1], at[1], sizes[1], widths[1])
        return pltpu.make_async_remote_copy(
            src_ref=ref.at[(*lead, pl.ds(si, ni), pl.ds(sj, nj))],
            dst_ref=ref.at[(*lead, pl.ds(ti, ni), pl.ds(tj, nj))],
            send_sem=send, recv_sem=recv, device_id=peer, device_id_type=MESH,
        )

    def stage_a(i, step, peer):
        at, sizes = (I0, J0), (W0, W0)
        if step[0] and step[1]:
            return [message(x0, (pl.ds(0, 3),), step, (2, 2), at, sizes, send_a.at[i, 0], recv_a.at[i, 0], peer)]
        return [
            message(x0, (pl.ds(0, 2),), step, (2, 2), at, sizes, send_a.at[i, 0], recv_a.at[i, 0], peer),
            message(x0, (2,), step, (3, 3), at, sizes, send_a.at[i, 1], recv_a.at[i, 1], peer),
        ]

    def stage_b(i, step, peer):
        rows = 3 if step[1] else 4
        return [message(x1, (pl.ds(0, 2),), step, (rows, W1), (I1, J1), (H1, W1), send_b.at[i], recv_b.at[i], peer)]

    def stage_c(i, step, peer):
        return [message(f1, (), step, (3, W1), (I1, J1), (H1, W1), send_c.at[i], recv_c.at[i], peer)]

    def each(stage, act, keep=lambda step: True):
        for i, step in enumerate(DIRS):
            if keep(step):
                ok, peer = reach(step)

                @pl.when(ok)
                def _():
                    for copy in stage(i, step, peer):
                        act(copy)

    def receive(stage, keep=lambda step: True):
        for i, step in reversed(list(enumerate(DIRS))):
            if keep(step):
                ok, peer = reach((-step[0], -step[1]))

                @pl.when(ok)
                def _():
                    for copy in stage(i, step, peer):
                        copy.wait_recv()

    def start(copy):
        copy.start()

    each(stage_a, start)
    each(stage_b, start)

    def diagonal(a, z):
        f, m, c = x0[0, a:z], x0[1, a:z], x0[2, a - 1 : z + 1]
        invd = inverse(m, c[1:-1], around(c, 1))
        y = f * invd
        inv0[a:z], y0[a:z], cy0[a:z] = invd, y, c[1:-1] * y

    def second(a, z):
        f, c = x0[0, a:z], x0[2, a:z]
        s = (0.125 * beta) * (c * around(y0[a - 1 : z + 1], 1) + around(cy0[a - 1 : z + 1], 1))
        x2 = inv0[a:z] * (alpha * f + s)
        x20[a:z], cx20[a:z], base0[a:z] = x2, c * x2, (1.0 - alpha) * f - s

    def residual(a, z):
        c = x0[2, a:z]
        total = c * around(x20[a - 1 : z + 1], 1) + around(cx20[a - 1 : z + 1], 1)
        r0[a:z] = (base0[a:z] + 0.125 * total)[:, J0 : J0 + W0]

    receive(stage_a, lambda step: step[0] == 0)
    diagonal(4, 18)
    second(5, 17)
    residual(6, 16)
    receive(stage_a, lambda step: step[0] == 1)
    diagonal(1, 4)
    second(2, 5)
    residual(3, 6)
    receive(stage_a, lambda step: step[0] == -1)
    diagonal(18, 21)
    second(17, 20)
    residual(16, 19)
    f1[own1] = pack_pool(r0[I0 : I0 + W0], pool0)
    each(stage_c, start)
    fine_ref[...] = x20[(pl.ds(I0, W0), pl.ds(J0, W0))]

    receive(stage_b)
    m1, c1 = x1[0], x1[1]
    c2 = unpack_pool(c1, pool1)
    m2 = unpack_pool(m1, pool1)
    invd1 = inverse(m1[1:-1], c1[1:-1], around_pairs(c1, 2))
    invd2 = inverse(m2[1:-1], c2[1:-1], around(c2, 4))
    each(stage_a, lambda copy: copy.wait_send())
    each(stage_b, lambda copy: copy.wait_send())

    receive(stage_c)
    f = f1[1:-1]
    y = f * invd1
    edge = jnp.zeros((1, *E1[1:]), jnp.float32)
    y = jnp.concatenate([edge, y, edge], axis=0)
    s = (0.125 * beta) * (c1[1:-1] * around_pairs(y, 2) + around_pairs(c1 * y, 2))
    x2 = invd1 * (alpha * f + s)
    middle = x2[3:7, J1 : J1 + W1]
    cx2 = c1[1:-1] * x2
    total = c1[2:-2] * around_pairs(x2, 2) + around_pairs(cx2, 2)
    r2 = (1.0 - alpha) * f[1:-1] - s[1:-1] + 0.125 * total

    f = unpack_pool(r2, pool1)
    c, invd = c2[2:10], invd2[1:9]
    y = f * invd
    s = (0.125 * beta) * (c[1:-1] * around(y, 4) + around(c * y, 4))
    x2 = invd[1:-1] * (alpha * f[1:-1] + s)
    coarse = x2[1:5, 4:8]
    total = c[2:-2] * around(x2, 4) + around(c[1:-1] * x2, 4)
    r2 = (1.0 - alpha) * f[2:-2] - s[1:-1] + 0.125 * total

    pool2[0], pool2[1] = r2[0] + r2[1], r2[2] + r2[3]
    both = pool2[:, pl.ds(4, 2, stride=2), :] + pool2[:, pl.ds(5, 2, stride=2), :]
    upper = both[0] + turn(both[0], -4)
    lower = turn(both[1], 1) + turn(both[1], -3)
    f3[...] = 0.125 * jnp.where(lanes_of(upper) % 2 == 0, upper, lower)

    def share(k, owner):
        return pltpu.make_async_remote_copy(
            src_ref=f3, dst_ref=gather_ref.at[owner], send_sem=send_d.at[k], recv_sem=recv_d.at[k],
            device_id=mate(k), device_id_type=MESH,
        )

    for k in mates:
        share(k, g).start()

    gather_ref[g] = f3[...]
    flat = middle.reshape(H1 * W1, LANES)
    for side in range(2):
        rows = squeeze(flat, 2, side).reshape(H1, W1, LANES // 2)
        for i in range(H1):
            middle_ref[2 * i + side] = rows[i]
    for i in range(4):
        coarse_ref[i] = squeeze(coarse[i], 4)

    each(stage_c, lambda copy: copy.wait_send())
    for k in mates:
        share(k, g).wait_send()
    for k in reversed(mates):
        share(k, lax.rem(g + groups - k, groups)).wait_recv()


def finish_kernel(fine, middle, coarse, gathered, fine_out, middle_out, coarse_out, rhs_out, rhs, sem):
    copies = [
        pltpu.make_async_copy(source, target, sem.at[i])
        for i, (source, target) in enumerate(((fine, fine_out), (middle, middle_out), (coarse, coarse_out)))
    ]
    for copy in copies:
        copy.start()
    depth = rhs.shape[1]
    row = lax.broadcasted_iota(jnp.int32, (2 * depth, LANES), 0)
    lane = lax.broadcasted_iota(jnp.int32, (2 * depth, LANES), 1)
    pick = lane == 8 * (row % depth) + row // depth
    both = lax.dot_general(
        pick.astype(jnp.float32), gathered[...].reshape(-1, LANES), (((1,), (1,)), ((), ())),
        precision=lax.Precision.HIGHEST, preferred_element_type=jnp.float32,
    )
    rhs[0], rhs[1] = both[:depth], both[depth:]
    last = pltpu.make_async_copy(rhs, rhs_out, sem.at[3])
    last.start()
    for copy in (*copies, last):
        copy.wait()


def solution(mesh):
    bricks, groups = mesh.shape["brick"], mesh.shape["group"]
    anywhere = pl.BlockSpec(memory_space=pl.ANY)
    vmem = pl.BlockSpec(memory_space=pltpu.VMEM)

    def buf(*shape):
        return pltpu.VMEM(shape, jnp.float32)

    dma = pltpu.SemaphoreType.DMA

    def body(right_side, mass_coef, face_coef):
        small = ((W0, W0, LANES), (W1, W1, LANES // 2), (4, 4, LANES // 4))
        held = pl.pallas_call(
            functools.partial(main_kernel, bricks, groups),
            out_shape=(*(buf(*shape) for shape in small), buf(groups, 2, LANES)),
            in_specs=[anywhere] * 3,
            out_specs=(vmem,) * 4,
            scratch_shapes=[
                buf(3, *E0), buf(2, *E1), buf(*E1),
                *([buf(*E0)] * 6), buf(E0[0], W0, LANES),
                buf(2, 4, W0, LANES), buf(12, 24, LANES), buf(2, 12, LANES), buf(2, LANES),
                dma((3,)), dma((8, 2)), dma((8, 2)), dma((8,)), dma((8,)), dma((8,)), dma((8,)),
                dma((groups,)), dma((groups,)),
            ],
            compiler_params=pltpu.CompilerParams(collective_id=0, has_side_effects=True),
            name="cycle",
        )(right_side, mass_coef, face_coef)
        held = [pltpu.with_memory_space_constraint(array, pltpu.VMEM) for array in held]
        rhs_shape = (2, LANES // 8, 2 * groups)
        fine, middle, coarse, rhs = pl.pallas_call(
            finish_kernel,
            out_shape=tuple(jax.ShapeDtypeStruct(shape, jnp.float32) for shape in (*small, rhs_shape)),
            in_specs=[vmem] * 4,
            out_specs=(anywhere,) * 4,
            scratch_shapes=[buf(*rhs_shape), dma((4,))],
            name="finish",
        )(*held)
        return fine, middle, coarse, jnp.swapaxes(rhs, 1, 2)

    placed = P("brick", "group", None)
    return jax.shard_map(
        body,
        mesh=mesh,
        in_specs=(placed, placed, placed),
        out_specs=(placed, placed, placed, P("brick", None, None)),
        check_vma=False,
    )
```

```python
import functools

import jax
import jax.numpy as jnp
from jax import lax
from jax.experimental import pallas as pl
from jax.experimental.pallas import tpu as pltpu
from jax.sharding import PartitionSpec as P

MESH = pl.DeviceIdType.MESH

center_value = 1.1
half_width = 0.8
ratio_sigma = center_value / half_width
first_rho = 1.0 / ratio_sigma
second_rho = 1.0 / (2.0 * ratio_sigma - first_rho)
carry_factor = second_rho * first_rho
push_factor = 2.0 * second_rho / half_width

alpha = (1.0 + carry_factor) / center_value + push_factor * (1.0 - 1.0 / center_value)
beta = push_factor / center_value

OUTSIDE_MASS = 1e30
LANES = 128
I0, J0, W0, E0 = 3, 8, 16, (22, 32, LANES)
I1, H1, J1, W1, E1 = 4, 4, 8, 8, (12, 24, LANES)

DIRS = [(1, 0), (-1, 0), (1, 1), (1, -1), (-1, 1), (-1, -1), (0, 1), (0, -1)]


def cut(step, start, size, width):
    if step == 0:
        return start, start, size
    if step > 0:
        return start + size - width, start - width, width
    return start, start + size, width


def lanes_of(a):
    return lax.broadcasted_iota(jnp.int32, a.shape, a.ndim - 1)


def turn(a, by):
    return pltpu.roll(a, by % LANES, axis=a.ndim - 1)


def beside(mid, by):
    lane = lanes_of(mid)
    low = jnp.where(lane >= by, turn(mid, by), 0.0)
    high = jnp.where(lane < LANES - by, turn(mid, -by), 0.0)
    cols = mid.shape[1]
    return low + high + pltpu.roll(mid, 1, axis=1) + pltpu.roll(mid, cols - 1, axis=1)


def around(a, by):
    return a[2:] + a[:-2] + beside(a[1:-1], by)


def around_pairs(a, by):
    up, down = turn(a[:-1], -1), turn(a[1:], 1)
    even = lanes_of(a[1:-1]) % 2 == 0
    return jnp.where(even, up[1:] + up[:-1], down[1:] + down[:-1]) + beside(a[1:-1], by)


def inverse(m, c, total):
    diag = m + 0.75 * c + 0.125 * total
    rough = pl.reciprocal(diag, approx=True)
    rough = rough * (2.0 - diag * rough)
    return rough * (2.0 - diag * rough)


def squeeze(a, by, first=0):
    shape = (LANES, LANES // by)
    pick = lax.broadcasted_iota(jnp.int32, shape, 0) == by * lax.broadcasted_iota(jnp.int32, shape, 1) + first
    return lax.dot(
        a, pick.astype(jnp.float32), precision=lax.Precision.HIGHEST, preferred_element_type=jnp.float32
    )


def halve(a, scratch):
    rows, cols, _ = a.shape
    scratch[0:rows, 0:cols, :] = a
    return scratch[0:rows, pl.ds(0, cols // 2, stride=2), :] + scratch[0:rows, pl.ds(1, cols // 2, stride=2), :]


def pack_pool(a, scratch):
    rows, cols, _ = a.shape
    quad = a.reshape(rows // 4, 4, cols, LANES)
    upper, lower = halve(quad[:, 0] + quad[:, 1], scratch.at[0]), halve(quad[:, 2] + quad[:, 3], scratch.at[1])
    even = lanes_of(upper) % 2 == 0
    return 0.125 * jnp.where(even, upper + turn(upper, -1), lower + turn(lower, 1))


def unpack_pool(a, scratch):
    both = halve(a, scratch)
    both = both + turn(both, -1)
    return 0.125 * (both + turn(both, -2))


def main_kernel(
    bricks, groups,
    f_ref, m_ref, c_ref,
    fine_ref, middle_ref, coarse_ref, gather_ref,
    x0, x1, f1, inv0, y0, cy0, x20, cx20, base0, r0, pool0, pool1, pool2, f3, tally,
    load_sem, send_sem, side_sem, recv_sem,
):
    b, g = lax.axis_index("brick"), lax.axis_index("group")
    barrier = pltpu.get_barrier_semaphore()

    def reach(step):
        db, dg = step
        ok = (b + db >= 0) & (b + db < bricks) & (g + dg >= 0) & (g + dg < groups)
        return ok, {"brick": b + db, "group": g + dg}

    def mate(k):
        return {"brick": b, "group": lax.rem(g + k, groups)}

    mates = sorted(range(1, groups), key=lambda k: (abs(2 * k - groups), k))

    expected = groups - 1
    for step in DIRS[:6]:
        ok, peer = reach(step)
        expected = expected + ok.astype(jnp.int32)

        @pl.when(ok)
        def _():
            pl.semaphore_signal(barrier, inc=1, device_id=peer, device_id_type=MESH)

    for k in mates:
        pl.semaphore_signal(barrier, inc=1, device_id=mate(k), device_id_type=MESH)

    loads = [
        pltpu.make_async_copy(ref, x0.at[i, pl.ds(I0, W0), pl.ds(J0, W0), :], load_sem)
        for i, ref in enumerate((f_ref, m_ref, c_ref))
    ]
    for copy in loads:
        copy.start()

    def drain(sem, rows):
        part = tally.at[pl.ds(0, rows)]
        pltpu.make_async_copy(part, part, sem).wait()

    def drain_by_place(sem, rows_of, keep=True):
        wide, deep = (b > 0) & (b < bricks - 1), (g > 0) & (g < groups - 1)
        for nb in (1, 2):
            for ng in (1, 2):
                here = (wide if nb == 2 else ~wide) & (deep if ng == 2 else ~deep)

                @pl.when(here & keep)
                def _():
                    drain(sem, rows_of(nb, ng))

    def blank(rows0, cols0, rows1, cols1):
        shape0, shape1 = (rows0.size, cols0.size, LANES), (rows1.size, cols1.size, LANES)
        for i, value in enumerate((0.0, OUTSIDE_MASS, 0.0)):
            x0[i, rows0, cols0, :] = jnp.full(shape0, value, jnp.float32)
        for i, value in enumerate((OUTSIDE_MASS, 0.0)):
            x1[i, rows1, cols1, :] = jnp.full(shape1, value, jnp.float32)
        f1[rows1, cols1, :] = jnp.zeros(shape1, jnp.float32)

    every = (pl.ds(0, E0[0]), pl.ds(0, E0[1]), pl.ds(0, E1[0]), pl.ds(0, E1[1]))

    @pl.when(b == 0)
    def _():
        blank(pl.ds(0, I0), every[1], pl.ds(0, I1), every[3])

    @pl.when(b == bricks - 1)
    def _():
        blank(pl.ds(I0 + W0, I0), every[1], pl.ds(I1 + H1, I1), every[3])

    @pl.when(g == 0)
    def _():
        blank(every[0], pl.ds(0, J0), every[2], pl.ds(0, J1))

    @pl.when(g == groups - 1)
    def _():
        blank(every[0], pl.ds(J0 + W0, J0), every[2], pl.ds(J1 + W1, J1))

    own0 = (pl.ds(I0, W0), pl.ds(J0, W0))
    drain(load_sem, 3 * W0 * W0)
    own1 = (pl.ds(I1, H1), pl.ds(J1, W1))
    x1[(0, *own1)] = pack_pool(x0[(1, *own0)], pool0)
    x1[(1, *own1)] = pack_pool(x0[(2, *own0)], pool0)

    pl.semaphore_wait(barrier, expected)

    def message(ref, lead, step, widths, at, sizes, send, recv, peer):
        si, ti, ni = cut(step[0], at[0], sizes[0], widths[0])
        sj, tj, nj = cut(step[1], at[1], sizes[1], widths[1])
        return pltpu.make_async_remote_copy(
            src_ref=ref.at[(*lead, pl.ds(si, ni), pl.ds(sj, nj))],
            dst_ref=ref.at[(*lead, pl.ds(ti, ni), pl.ds(tj, nj))],
            send_sem=send, recv_sem=recv, device_id=peer, device_id_type=MESH,
        )

    def side_of(step):
        return side_sem.at[step[0] % 3]

    def stage_a(step, peer):
        widths = (2, 2) if step[0] and step[1] else (3, 3)
        return message(x0, (pl.ds(0, 3),), step, widths, (I0, J0), (W0, W0), send_sem.at[0], side_of(step), peer)

    def stage_b(step, peer):
        rows = 3 if step[1] else 4
        return message(
            x1, (pl.ds(0, 2),), step, (rows, W1), (I1, J1), (H1, W1), send_sem.at[1], recv_sem.at[0], peer
        )

    def stage_c(step, peer):
        return message(f1, (), step, (3, W1), (I1, J1), (H1, W1), send_sem.at[2], recv_sem.at[1], peer)

    size_a, size_b, size_c = (9 * W0, 9 * W0, 12), (8 * W1, 8 * W1, 6 * W1), (3 * W1, 4 * W1, 3 * W1)

    def all_of(size):
        return lambda nb, ng: nb * size[0] + ng * size[1] + nb * ng * size[2]

    def each(stage):
        for step in DIRS:
            ok, peer = reach(step)

            @pl.when(ok)
            def _():
                stage(step, peer).start()

    each(stage_a)
    each(stage_b)

    def diagonal(a, z):
        f, m, c = x0[0, a:z], x0[1, a:z], x0[2, a - 1 : z + 1]
        invd = inverse(m, c[1:-1], around(c, 1))
        y = f * invd
        inv0[a:z], y0[a:z], cy0[a:z] = invd, y, c[1:-1] * y

    def second(a, z):
        f, c = x0[0, a:z], x0[2, a:z]
        s = (0.125 * beta) * (c * around(y0[a - 1 : z + 1], 1) + around(cy0[a - 1 : z + 1], 1))
        x2 = inv0[a:z] * (alpha * f + s)
        x20[a:z], cx20[a:z], base0[a:z] = x2, c * x2, (1.0 - alpha) * f - s

    def residual(a, z):
        c = x0[2, a:z]
        total = c * around(x20[a - 1 : z + 1], 1) + around(cx20[a - 1 : z + 1], 1)
        r0[a:z] = (base0[a:z] + 0.125 * total)[:, J0 : J0 + W0]

    drain_by_place(side_sem.at[0], lambda nb, ng: ng * size_a[1])
    diagonal(4, 18)
    second(5, 17)
    residual(6, 16)
    drain_by_place(side_sem.at[1], lambda nb, ng: size_a[0] + ng * size_a[2], b > 0)
    diagonal(1, 4)
    second(2, 5)
    residual(3, 6)
    drain_by_place(side_sem.at[2], lambda nb, ng: size_a[0] + ng * size_a[2], b < bricks - 1)
    diagonal(18, 21)
    second(17, 20)
    residual(16, 19)
    f1[own1] = pack_pool(r0[I0 : I0 + W0], pool0)
    each(stage_c)
    fine_ref[...] = x20[(pl.ds(I0, W0), pl.ds(J0, W0))]

    drain_by_place(recv_sem.at[0], all_of(size_b))
    m1, c1 = x1[0], x1[1]
    c2 = unpack_pool(c1, pool1)
    m2 = unpack_pool(m1, pool1)
    invd1 = inverse(m1[1:-1], c1[1:-1], around_pairs(c1, 2))
    invd2 = inverse(m2[1:-1], c2[1:-1], around(c2, 4))
    drain_by_place(send_sem.at[0], all_of(size_a))
    drain_by_place(send_sem.at[1], all_of(size_b))

    drain_by_place(recv_sem.at[1], all_of(size_c))
    f = f1[1:-1]
    y = f * invd1
    edge = jnp.zeros((1, *E1[1:]), jnp.float32)
    y = jnp.concatenate([edge, y, edge], axis=0)
    s = (0.125 * beta) * (c1[1:-1] * around_pairs(y, 2) + around_pairs(c1 * y, 2))
    x2 = invd1 * (alpha * f + s)
    middle = x2[3:7, J1 : J1 + W1]
    cx2 = c1[1:-1] * x2
    total = c1[2:-2] * around_pairs(x2, 2) + around_pairs(cx2, 2)
    r2 = (1.0 - alpha) * f[1:-1] - s[1:-1] + 0.125 * total

    f = unpack_pool(r2, pool1)
    c, invd = c2[2:10], invd2[1:9]
    y = f * invd
    s = (0.125 * beta) * (c[1:-1] * around(y, 4) + around(c * y, 4))
    x2 = invd[1:-1] * (alpha * f[1:-1] + s)
    coarse = x2[1:5, 4:8]
    total = c[2:-2] * around(x2, 4) + around(c[1:-1] * x2, 4)
    r2 = (1.0 - alpha) * f[2:-2] - s[1:-1] + 0.125 * total

    pool2[0], pool2[1] = r2[0] + r2[1], r2[2] + r2[3]
    both = pool2[:, pl.ds(4, 2, stride=2), :] + pool2[:, pl.ds(5, 2, stride=2), :]
    upper = both[0] + turn(both[0], -4)
    lower = turn(both[1], 1) + turn(both[1], -3)
    f3[...] = 0.125 * jnp.where(lanes_of(upper) % 2 == 0, upper, lower)

    for k in mates:
        pltpu.make_async_remote_copy(
            src_ref=f3, dst_ref=gather_ref.at[g], send_sem=send_sem.at[3], recv_sem=recv_sem.at[2],
            device_id=mate(k), device_id_type=MESH,
        ).start()

    gather_ref[g] = f3[...]
    flat = middle.reshape(H1 * W1, LANES)
    for side in range(2):
        rows = squeeze(flat, 2, side).reshape(H1, W1, LANES // 2)
        for i in range(H1):
            middle_ref[2 * i + side] = rows[i]
    for i in range(4):
        coarse_ref[i] = squeeze(coarse[i], 4)

    drain_by_place(send_sem.at[2], all_of(size_c))
    drain(send_sem.at[3], 2 * (groups - 1))
    drain(recv_sem.at[2], 2 * (groups - 1))


def finish_kernel(fine, middle, coarse, gathered, fine_out, middle_out, coarse_out, rhs_out, rhs, sem):
    copies = [
        pltpu.make_async_copy(source, target, sem.at[i])
        for i, (source, target) in enumerate(((fine, fine_out), (middle, middle_out), (coarse, coarse_out)))
    ]
    for copy in copies:
        copy.start()
    depth = rhs.shape[1]
    row = lax.broadcasted_iota(jnp.int32, (2 * depth, LANES), 0)
    lane = lax.broadcasted_iota(jnp.int32, (2 * depth, LANES), 1)
    pick = lane == 8 * (row % depth) + row // depth
    both = lax.dot_general(
        pick.astype(jnp.float32), gathered[...].reshape(-1, LANES), (((1,), (1,)), ((), ())),
        precision=lax.Precision.HIGHEST, preferred_element_type=jnp.float32,
    )
    rhs[0], rhs[1] = both[:depth], both[depth:]
    last = pltpu.make_async_copy(rhs, rhs_out, sem.at[3])
    last.start()
    for copy in (*copies, last):
        copy.wait()


def solution(mesh):
    bricks, groups = mesh.shape["brick"], mesh.shape["group"]
    anywhere = pl.BlockSpec(memory_space=pl.ANY)
    vmem = pl.BlockSpec(memory_space=pltpu.VMEM)

    def buf(*shape):
        return pltpu.VMEM(shape, jnp.float32)

    dma = pltpu.SemaphoreType.DMA

    def body(right_side, mass_coef, face_coef):
        small = ((W0, W0, LANES), (W1, W1, LANES // 2), (4, 4, LANES // 4))
        held = pl.pallas_call(
            functools.partial(main_kernel, bricks, groups),
            out_shape=(*(buf(*shape) for shape in small), buf(groups, 2, LANES)),
            in_specs=[anywhere] * 3,
            out_specs=(vmem,) * 4,
            scratch_shapes=[
                buf(3, *E0), buf(2, *E1), buf(*E1),
                *([buf(*E0)] * 6), buf(E0[0], W0, LANES),
                buf(2, 4, W0, LANES), buf(12, 24, LANES), buf(2, 12, LANES), buf(2, LANES),
                buf(3 * W0 * W0, LANES), dma, dma((4,)), dma((3,)), dma((3,)),
            ],
            compiler_params=pltpu.CompilerParams(collective_id=0, has_side_effects=True),
            name="cycle",
        )(right_side, mass_coef, face_coef)
        held = [pltpu.with_memory_space_constraint(array, pltpu.VMEM) for array in held]
        rhs_shape = (2, LANES // 8, 2 * groups)
        fine, middle, coarse, rhs = pl.pallas_call(
            finish_kernel,
            out_shape=tuple(jax.ShapeDtypeStruct(shape, jnp.float32) for shape in (*small, rhs_shape)),
            in_specs=[vmem] * 4,
            out_specs=(anywhere,) * 4,
            scratch_shapes=[buf(*rhs_shape), dma((4,))],
            name="finish",
        )(*held)
        return fine, middle, coarse, jnp.swapaxes(rhs, 1, 2)

    placed = P("brick", "group", None)
    return jax.shard_map(
        body,
        mesh=mesh,
        in_specs=(placed, placed, placed),
        out_specs=(placed, placed, placed, P("brick", None, None)),
        check_vma=False,
    )
```

```python
import functools

import jax
import jax.numpy as jnp
from jax import lax
from jax.experimental import pallas as pl
from jax.experimental.pallas import tpu as pltpu
from jax.sharding import PartitionSpec as P

MESH = pl.DeviceIdType.MESH

center_value = 1.1
half_width = 0.8
ratio_sigma = center_value / half_width
first_rho = 1.0 / ratio_sigma
second_rho = 1.0 / (2.0 * ratio_sigma - first_rho)
carry_factor = second_rho * first_rho
push_factor = 2.0 * second_rho / half_width

alpha = (1.0 + carry_factor) / center_value + push_factor * (1.0 - 1.0 / center_value)
beta = push_factor / center_value

OUTSIDE_MASS = 1e30
LANES = 128
I0, J0, W0, E0 = 3, 12, 16, (22, 40, LANES)
J8 = pl.ds(8, 24)
I1, H1, J1, W1, E1 = 4, 4, 8, 8, (12, 24, LANES)

DIRS = [(1, 1), (1, -1), (-1, 1), (-1, -1), (1, 0), (-1, 0), (0, 1), (0, -1)]


def cut(step, start, size, width):
    if step == 0:
        return start, start, size
    if step > 0:
        return start + size - width, start - width, width
    return start, start + size, width


def lanes_of(a):
    return lax.broadcasted_iota(jnp.int32, a.shape, a.ndim - 1)


def turn(a, by):
    return pltpu.roll(a, by % LANES, axis=a.ndim - 1)


def beside(mid, by):
    lane = lanes_of(mid)
    low = jnp.where(lane >= by, turn(mid, by), 0.0)
    high = jnp.where(lane < LANES - by, turn(mid, -by), 0.0)
    cols = mid.shape[1]
    return low + high + pltpu.roll(mid, 1, axis=1) + pltpu.roll(mid, cols - 1, axis=1)


def around_at(ref, at, n):
    mid = ref[pl.ds(at, n), J8]
    lane = lanes_of(mid)
    low, high = jnp.where(lane >= 1, turn(mid, 1), 0.0), jnp.where(lane < LANES - 1, turn(mid, -1), 0.0)
    rows = ref[pl.ds(at - 1, n), J8] + ref[pl.ds(at + 1, n), J8]
    return rows + (ref[pl.ds(at, n), pl.ds(7, 24)] + ref[pl.ds(at, n), pl.ds(9, 24)]) + (low + high)


def around(a, by):
    return a[2:] + a[:-2] + beside(a[1:-1], by)


def rows_beside(a):
    return a[:-2], a[2:]


def pairs_beside(a):
    up, down = turn(a[:-1], -1), turn(a[1:], 1)
    even = lanes_of(a[1:-1]) % 2 == 0
    return jnp.where(even, up[:-1], down[:-1]), jnp.where(even, up[1:], down[1:])


def six(a, by, rows):
    mid = a[1:-1]
    return (
        *rows(a), pltpu.roll(mid, 1, axis=1), pltpu.roll(mid, mid.shape[1] - 1, axis=1), turn(mid, by), turn(mid, -by)
    )


def weigh(c, by, rows, out):
    mid = c[1:-1]
    lane = lanes_of(mid)
    total = None
    for i, near in enumerate(six(c, by, rows)):
        inside = {4: lane >= by, 5: lane < LANES - by}.get(i)
        if inside is not None:
            near = jnp.where(inside, near, 0.0)
        weight = 0.125 * (mid + near)
        out[i] = weight if inside is None else jnp.where(inside, weight, 0.0)
        total = near if total is None else total + near
    return total


def spread(u, by, rows, weights):
    near = six(u, by, rows)
    parts = [weights(i) * near[i] for i in range(6)]
    return ((parts[0] + parts[1]) + (parts[2] + parts[3])) + (parts[4] + parts[5])


def inverse(m, c, total):
    diag = m + 0.75 * c + 0.125 * total
    rough = pl.reciprocal(diag, approx=True)
    rough = rough * (2.0 - diag * rough)
    return rough * (2.0 - diag * rough)


def squeeze(a, by, first=0):
    shape = (LANES, LANES // by)
    pick = lax.broadcasted_iota(jnp.int32, shape, 0) == by * lax.broadcasted_iota(jnp.int32, shape, 1) + first
    return lax.dot(
        a, pick.astype(jnp.float32), precision=lax.Precision.HIGHEST, preferred_element_type=jnp.float32
    )


def halve(a, scratch, first=0, count=None):
    rows, cols, _ = a.shape
    count = count or cols // 2
    scratch[0:rows, 0:cols, :] = a
    even, odd = pl.ds(first, count, stride=2), pl.ds(first + 1, count, stride=2)
    return scratch[0:rows, even, :] + scratch[0:rows, odd, :]


def pack_pool(a, scratch, first=0):
    rows, cols, _ = a.shape
    quad = a.reshape(rows // 4, 4, cols, LANES)
    upper = halve(quad[:, 0] + quad[:, 1], scratch.at[0], first, W1)
    lower = halve(quad[:, 2] + quad[:, 3], scratch.at[1], first, W1)
    even = lanes_of(upper) % 2 == 0
    return 0.125 * jnp.where(even, upper + turn(upper, -1), lower + turn(lower, 1))


def unpack_pool(a, scratch):
    both = halve(a, scratch)
    both = both + turn(both, -1)
    return 0.125 * (both + turn(both, -2))


def main_kernel(
    bricks, groups,
    f_ref, m_ref, c_ref,
    fine_ref, middle_ref, coarse_ref, gather_ref,
    x0, x1, f1, inv0, y0, cy0, x20, cx20, base0, r0, pool0, pool1, pool2, f3, tally, w1, w2, invd1, invd2,
    load_sem, send_sem, side_sem, recv_sem, word_sem,
):
    b, g = lax.axis_index("brick"), lax.axis_index("group")
    barrier = pltpu.get_barrier_semaphore()

    def reach(step):
        db, dg = step
        ok = (b + db >= 0) & (b + db < bricks) & (g + dg >= 0) & (g + dg < groups)
        return ok, {"brick": b + db, "group": g + dg}

    def mate(k):
        return {"brick": b, "group": lax.rem(g + k, groups)}

    mates = sorted(range(1, groups), key=lambda k: (abs(2 * k - groups), k))

    expected = 2
    for step in DIRS[:6]:
        ok, peer = reach(step)
        expected = expected + ok.astype(jnp.int32)

        @pl.when(ok)
        def _():
            pl.semaphore_signal(barrier, inc=1, device_id=peer, device_id_type=MESH)

    for k in (1, groups - 1):
        pl.semaphore_signal(barrier, inc=1, device_id=mate(k), device_id_type=MESH)

    hops = []
    while 2 ** len(hops) < groups // 2:
        hops.append(2 ** len(hops))

    def tell(i):
        if i < len(hops):
            for k in (hops[i], groups - hops[i]):
                pl.semaphore_signal(word_sem.at[i], inc=1, device_id=mate(k), device_id_type=MESH)

    def hear(i):
        if i < len(hops):
            pl.semaphore_wait(word_sem.at[i], 2)

    loads = [
        pltpu.make_async_copy(ref, x0.at[i, pl.ds(I0, W0), pl.ds(J0, W0), :], load_sem)
        for i, ref in enumerate((f_ref, m_ref, c_ref))
    ]
    for copy in loads:
        copy.start()

    def drain(sem, rows):
        part = tally.at[pl.ds(0, rows)]
        pltpu.make_async_copy(part, part, sem).wait()

    def drain_by_place(sem, rows_of, keep=True):
        wide, deep = (b > 0) & (b < bricks - 1), (g > 0) & (g < groups - 1)
        for nb in (1, 2):
            for ng in (1, 2):
                here = (wide if nb == 2 else ~wide) & (deep if ng == 2 else ~deep)

                @pl.when(here & keep)
                def _():
                    drain(sem, rows_of(nb, ng))

    def blank(rows0, cols0, rows1, cols1):
        shape0, shape1 = (rows0.size, cols0.size, LANES), (rows1.size, cols1.size, LANES)
        for i, value in enumerate((0.0, OUTSIDE_MASS, 0.0)):
            x0[i, rows0, cols0, :] = jnp.full(shape0, value, jnp.float32)
        for i, value in enumerate((OUTSIDE_MASS, 0.0)):
            x1[i, rows1, cols1, :] = jnp.full(shape1, value, jnp.float32)
        f1[rows1, cols1, :] = jnp.zeros(shape1, jnp.float32)

    every = (pl.ds(0, E0[0]), pl.ds(0, E0[1]), pl.ds(0, E1[0]), pl.ds(0, E1[1]))

    @pl.when(b == 0)
    def _():
        blank(pl.ds(0, I0), every[1], pl.ds(0, I1), every[3])

    @pl.when(b == bricks - 1)
    def _():
        blank(pl.ds(I0 + W0, I0), every[1], pl.ds(I1 + H1, I1), every[3])

    @pl.when(g == 0)
    def _():
        blank(every[0], pl.ds(0, J0), every[2], pl.ds(0, J1))

    @pl.when(g == groups - 1)
    def _():
        blank(every[0], pl.ds(J0 + W0, J0), every[2], pl.ds(J1 + W1, J1))

    own0 = (pl.ds(I0, W0), pl.ds(J0, W0))
    drain(load_sem, 3 * W0 * W0)
    own1 = (pl.ds(I1, H1), pl.ds(J1, W1))
    x1[(0, *own1)] = pack_pool(x0[(1, *own0)], pool0)
    x1[(1, *own1)] = pack_pool(x0[(2, *own0)], pool0)

    pl.semaphore_wait(barrier, expected)

    def message(ref, lead, step, widths, at, sizes, send, recv, peer):
        si, ti, ni = cut(step[0], at[0], sizes[0], widths[0])
        sj, tj, nj = cut(step[1], at[1], sizes[1], widths[1])
        return pltpu.make_async_remote_copy(
            src_ref=ref.at[(*lead, pl.ds(si, ni), pl.ds(sj, nj))],
            dst_ref=ref.at[(*lead, pl.ds(ti, ni), pl.ds(tj, nj))],
            send_sem=send, recv_sem=recv, device_id=peer, device_id_type=MESH,
        )

    def side_of(step):
        return side_sem.at[step[0] % 3]

    def stage_a(step, peer):
        def part(lead, width):
            return message(
                x0, (lead,), step, (width, width), (I0, J0), (W0, W0), send_sem.at[0], side_of(step), peer
            )

        return [part(pl.ds(0, 3), 2)] if step[0] and step[1] else [part(pl.ds(0, 2), 2), part(2, 3)]

    def stage_b(step, peer):
        rows = 3 if step[1] else 4
        return [message(
            x1, (pl.ds(0, 2),), step, (rows, W1), (I1, J1), (H1, W1), send_sem.at[1], recv_sem.at[0], peer
        )]

    def stage_c(step, peer):
        return [message(f1, (), step, (3, W1), (I1, J1), (H1, W1), send_sem.at[2], recv_sem.at[1], peer)]

    size_a, size_b, size_c = (7 * W0, 7 * W0, 12), (8 * W1, 8 * W1, 6 * W1), (3 * W1, 4 * W1, 3 * W1)

    def all_of(size):
        return lambda nb, ng: nb * size[0] + ng * size[1] + nb * ng * size[2]

    def each(stage):
        for step in DIRS:
            ok, peer = reach(step)

            @pl.when(ok)
            def _():
                for copy in stage(step, peer):
                    copy.start()

    tell(0)
    each(stage_a)
    each(stage_b)
    hear(0)
    tell(1)

    def diagonal(at, n):
        rows = pl.ds(at, n)
        f, m, c = x0[0, rows, J8], x0[1, rows, J8], x0[2, rows, J8]
        invd = inverse(m, c, around_at(x0.at[2], at, n))
        y = f * invd
        inv0[rows, J8], y0[rows, J8], cy0[rows, J8] = invd, y, c * y

    def second(at, n):
        rows = pl.ds(at, n)
        f, c = x0[0, rows, J8], x0[2, rows, J8]
        s = (0.125 * beta) * (c * around_at(y0, at, n) + around_at(cy0, at, n))
        x2 = inv0[rows, J8] * (alpha * f + s)
        x20[rows, J8], cx20[rows, J8], base0[rows, J8] = x2, c * x2, (1.0 - alpha) * f - s

    def residual(at, n):
        rows = pl.ds(at, n)
        total = x0[2, rows, J8] * around_at(x20, at, n) + around_at(cx20, at, n)
        r0[rows] = base0[rows, J8] + 0.125 * total

    drain_by_place(side_sem.at[0], lambda nb, ng: ng * size_a[1])
    diagonal(4, 14)
    second(5, 12)
    residual(6, 10)
    f1[pl.ds(I1 + 1, 2), pl.ds(J1, W1), :] = pack_pool(r0[7:15], pool0, J0 - 8)
    hear(1)
    tell(2)
    run = 4
    for turn_no in range(2):
        low = (lax.rem(b, run) != 0) if turn_no == 0 else (lax.rem(b, run) == 0)

        def arrived(nb, ng):
            return size_a[0] + ng * size_a[2]

        drain_by_place(side_sem.at[1], arrived, low & (b > 0))
        drain_by_place(side_sem.at[2], arrived, ~low & (b < bricks - 1))
        diagonal(jnp.where(low, 1, 18), 3)
        second(jnp.where(low, 2, 17), 3)
        residual(jnp.where(low, 3, 16), 3)
        quad = pack_pool(r0[pl.ds(jnp.where(low, 3, 15), 4)], pool0, J0 - 8)
        f1[pl.ds(jnp.where(low, I1, I1 + 3), 1), pl.ds(J1, W1), :] = quad
    each(stage_c)
    fine_ref[...] = x20[own0]

    drain_by_place(recv_sem.at[0], all_of(size_b))
    m1, c1 = x1[0], x1[1]
    c2 = unpack_pool(c1, pool1)
    m2 = unpack_pool(m1, pool1)
    invd1[...] = inverse(m1[1:-1], c1[1:-1], weigh(c1, 2, pairs_beside, w1))
    invd2[...] = inverse(m2[1:-1], c2[1:-1], weigh(c2, 4, rows_beside, w2))
    drain_by_place(send_sem.at[0], all_of(size_a))
    drain_by_place(send_sem.at[1], all_of(size_b))

    drain_by_place(recv_sem.at[1], all_of(size_c))
    f = f1[1:-1]
    invd = invd1[...]
    edge = jnp.zeros((1, *E1[1:]), jnp.float32)
    y = jnp.concatenate([edge, f * invd, edge], axis=0)
    s = beta * spread(y, 2, pairs_beside, lambda i: w1[i])
    x2 = invd * (alpha * f + s)
    middle = x2[3:7, J1 : J1 + W1]
    r2 = (1.0 - alpha) * f[1:-1] - s[1:-1] + spread(x2, 2, pairs_beside, lambda i: w1[i, 1:9])

    f = unpack_pool(r2, pool1)
    invd = invd2[1:9]
    s = beta * spread(f * invd, 4, rows_beside, lambda i: w2[i, 2:8])
    x2 = invd[1:-1] * (alpha * f[1:-1] + s)
    coarse = x2[1:5, 4:8]
    r2 = (1.0 - alpha) * f[2:-2] - s[1:-1] + spread(x2, 4, rows_beside, lambda i: w2[i, 3:7])

    pool2[0], pool2[1] = r2[0] + r2[1], r2[2] + r2[3]
    both = pool2[:, pl.ds(4, 2, stride=2), :] + pool2[:, pl.ds(5, 2, stride=2), :]
    upper = both[0] + turn(both[0], -4)
    lower = turn(both[1], 1) + turn(both[1], -3)
    f3[...] = 0.125 * jnp.where(lanes_of(upper) % 2 == 0, upper, lower)

    hear(2)
    for k in mates:
        pltpu.make_async_remote_copy(
            src_ref=f3, dst_ref=gather_ref.at[g], send_sem=send_sem.at[3], recv_sem=recv_sem.at[2],
            device_id=mate(k), device_id_type=MESH,
        ).start()

    gather_ref[g] = f3[...]
    flat = middle.reshape(H1 * W1, LANES)
    for side in range(2):
        rows = squeeze(flat, 2, side).reshape(H1, W1, LANES // 2)
        for i in range(H1):
            middle_ref[2 * i + side] = rows[i]
    for i in range(4):
        coarse_ref[i] = squeeze(coarse[i], 4)

    drain_by_place(send_sem.at[2], all_of(size_c))
    drain(send_sem.at[3], 2 * (groups - 1))
    drain(recv_sem.at[2], 2 * (groups - 1))


def finish_kernel(fine, middle, coarse, gathered, fine_out, middle_out, coarse_out, rhs_out, rhs, sem):
    copies = [
        pltpu.make_async_copy(source, target, sem.at[i])
        for i, (source, target) in enumerate(((fine, fine_out), (middle, middle_out), (coarse, coarse_out)))
    ]
    for copy in copies:
        copy.start()
    depth = rhs.shape[1]
    row = lax.broadcasted_iota(jnp.int32, (2 * depth, LANES), 0)
    lane = lax.broadcasted_iota(jnp.int32, (2 * depth, LANES), 1)
    pick = lane == 8 * (row % depth) + row // depth
    both = lax.dot_general(
        pick.astype(jnp.float32), gathered[...].reshape(-1, LANES), (((1,), (1,)), ((), ())),
        precision=lax.Precision.HIGHEST, preferred_element_type=jnp.float32,
    )
    rhs[0], rhs[1] = both[:depth], both[depth:]
    last = pltpu.make_async_copy(rhs, rhs_out, sem.at[3])
    last.start()
    for copy in (*copies, last):
        copy.wait()


def solution(mesh):
    bricks, groups = mesh.shape["brick"], mesh.shape["group"]
    anywhere = pl.BlockSpec(memory_space=pl.ANY)
    vmem = pl.BlockSpec(memory_space=pltpu.VMEM)

    def buf(*shape):
        return pltpu.VMEM(shape, jnp.float32)

    dma = pltpu.SemaphoreType.DMA

    def body(right_side, mass_coef, face_coef):
        small = ((W0, W0, LANES), (W1, W1, LANES // 2), (4, 4, LANES // 4))
        held = pl.pallas_call(
            functools.partial(main_kernel, bricks, groups),
            out_shape=(*(buf(*shape) for shape in small), buf(groups, 2, LANES)),
            in_specs=[anywhere] * 3,
            out_specs=(vmem,) * 4,
            scratch_shapes=[
                buf(3, *E0), buf(2, *E1), buf(*E1),
                *([buf(*E0)] * 6), buf(E0[0], 24, LANES),
                buf(2, 4, 24, LANES), buf(12, 24, LANES), buf(2, 12, LANES), buf(2, LANES),
                buf(3 * W0 * W0, LANES),
                buf(6, 10, 24, LANES), buf(6, 10, 12, LANES), buf(10, 24, LANES), buf(10, 12, LANES),
                dma, dma((4,)), dma((3,)), dma((3,)), pltpu.SemaphoreType.REGULAR((3,)),
            ],
            compiler_params=pltpu.CompilerParams(collective_id=0, has_side_effects=True),
            name="cycle",
        )(right_side, mass_coef, face_coef)
        held = [pltpu.with_memory_space_constraint(array, pltpu.VMEM) for array in held]
        rhs_shape = (2, LANES // 8, 2 * groups)
        fine, middle, coarse, rhs = pl.pallas_call(
            finish_kernel,
            out_shape=tuple(jax.ShapeDtypeStruct(shape, jnp.float32) for shape in (*small, rhs_shape)),
            in_specs=[vmem] * 4,
            out_specs=(anywhere,) * 4,
            scratch_shapes=[buf(*rhs_shape), dma((4,))],
            name="finish",
        )(*held)
        return fine, middle, coarse, jnp.swapaxes(rhs, 1, 2)

    placed = P("brick", "group", None)
    return jax.shard_map(
        body,
        mesh=mesh,
        in_specs=(placed, placed, placed),
        out_specs=(placed, placed, placed, P("brick", None, None)),
        check_vma=False,
    )
```

```python
import functools

import jax
import jax.numpy as jnp
from jax import lax
from jax.experimental import pallas as pl
from jax.experimental.pallas import tpu as pltpu
from jax.sharding import PartitionSpec as P

MESH = pl.DeviceIdType.MESH

center_value = 1.1
half_width = 0.8
ratio_sigma = center_value / half_width
first_rho = 1.0 / ratio_sigma
second_rho = 1.0 / (2.0 * ratio_sigma - first_rho)
carry_factor = second_rho * first_rho
push_factor = 2.0 * second_rho / half_width

alpha = (1.0 + carry_factor) / center_value + push_factor * (1.0 - 1.0 / center_value)
beta = push_factor / center_value

OUTSIDE_MASS = 1e30
LANES = 128
I0, J0, W0, E0 = 3, 12, 16, (22, 40, LANES)
J8 = pl.ds(8, 24)
K0, PATCH = 3, (10, 16, LANES)
J4 = pl.ds(4, 8)
CORNERS = [(1, 1), (1, 0), (0, 1), (0, 0)]
I1, H1, J1, W1, E1 = 4, 4, 8, 8, (12, 24, LANES)

DIRS = [(1, 1), (1, -1), (-1, 1), (-1, -1), (1, 0), (-1, 0), (0, 1), (0, -1)]


def cut(step, start, size, width, skip):
    if step == 0:
        return start, start, size
    if step > 0:
        return start + size - width - skip, start - width - skip, width
    return start + skip, start + size + skip, width


def lanes_of(a):
    return lax.broadcasted_iota(jnp.int32, a.shape, a.ndim - 1)


def turn(a, by):
    return pltpu.roll(a, by % LANES, axis=a.ndim - 1)


def beside(mid, by):
    lane = lanes_of(mid)
    low = jnp.where(lane >= by, turn(mid, by), 0.0)
    high = jnp.where(lane < LANES - by, turn(mid, -by), 0.0)
    cols = mid.shape[1]
    return low + high + pltpu.roll(mid, 1, axis=1) + pltpu.roll(mid, cols - 1, axis=1)


def around_at(ref, at, n, cols):
    rows = pl.ds(at, n)
    mid = ref[rows, cols]
    lane = lanes_of(mid)
    low, high = jnp.where(lane >= 1, turn(mid, 1), 0.0), jnp.where(lane < LANES - 1, turn(mid, -1), 0.0)
    left, right = pl.ds(cols.start - 1, cols.size), pl.ds(cols.start + 1, cols.size)
    return ref[pl.ds(at - 1, n), cols] + ref[pl.ds(at + 1, n), cols] + (ref[rows, left] + ref[rows, right]) + (low + high)


def around(a, by):
    return a[2:] + a[:-2] + beside(a[1:-1], by)


def rows_beside(a):
    return a[:-2], a[2:]


def pairs_beside(a):
    up, down = turn(a[:-1], -1), turn(a[1:], 1)
    even = lanes_of(a[1:-1]) % 2 == 0
    return jnp.where(even, up[:-1], down[:-1]), jnp.where(even, up[1:], down[1:])


def six(a, by, rows):
    mid = a[1:-1]
    return (
        *rows(a), pltpu.roll(mid, 1, axis=1), pltpu.roll(mid, mid.shape[1] - 1, axis=1), turn(mid, by), turn(mid, -by)
    )


def weigh(c, by, rows, out):
    mid = c[1:-1]
    lane = lanes_of(mid)
    total = None
    for i, near in enumerate(six(c, by, rows)):
        inside = {4: lane >= by, 5: lane < LANES - by}.get(i)
        if inside is not None:
            near = jnp.where(inside, near, 0.0)
        weight = 0.125 * (mid + near)
        out[i] = weight if inside is None else jnp.where(inside, weight, 0.0)
        total = near if total is None else total + near
    return total


def spread(u, by, rows, weights):
    near = six(u, by, rows)
    parts = [weights(i) * near[i] for i in range(6)]
    return ((parts[0] + parts[1]) + (parts[2] + parts[3])) + (parts[4] + parts[5])


def inverse(m, c, total):
    diag = m + 0.75 * c + 0.125 * total
    rough = pl.reciprocal(diag, approx=True)
    rough = rough * (2.0 - diag * rough)
    return rough * (2.0 - diag * rough)


def squeeze(a, by, first=0):
    shape = (LANES, LANES // by)
    pick = lax.broadcasted_iota(jnp.int32, shape, 0) == by * lax.broadcasted_iota(jnp.int32, shape, 1) + first
    return lax.dot(
        a, pick.astype(jnp.float32), precision=lax.Precision.HIGHEST, preferred_element_type=jnp.float32
    )


def halve(a, scratch, first=0, count=None):
    rows, cols, _ = a.shape
    count = count or cols // 2
    scratch[0:rows, 0:cols, :] = a
    even, odd = pl.ds(first, count, stride=2), pl.ds(first + 1, count, stride=2)
    return scratch[0:rows, even, :] + scratch[0:rows, odd, :]


def pack_pool(a, scratch, first=0):
    rows, cols, _ = a.shape
    quad = a.reshape(rows // 4, 4, cols, LANES)
    upper = halve(quad[:, 0] + quad[:, 1], scratch.at[0], first, W1)
    lower = halve(quad[:, 2] + quad[:, 3], scratch.at[1], first, W1)
    even = lanes_of(upper) % 2 == 0
    return 0.125 * jnp.where(even, upper + turn(upper, -1), lower + turn(lower, 1))


def unpack_pool(a, scratch):
    both = halve(a, scratch)
    both = both + turn(both, -1)
    return 0.125 * (both + turn(both, -2))


def main_kernel(
    bricks, groups,
    f_ref, m_ref, c_ref,
    fine_ref, middle_ref, coarse_ref, gather_ref,
    x0, x1, f1, inv0, y0, cy0, x20, cx20, base0, r0, pool0, pool1, pool2, f3, tally, w1, w2, invd1, invd2, px, work, pool3, near,
    load_sem, send_sem, side_sem, recv_sem, word_sem,
):
    b, g = lax.axis_index("brick"), lax.axis_index("group")
    barrier = pltpu.get_barrier_semaphore()

    def reach(step):
        db, dg = step
        ok = (b + db >= 0) & (b + db < bricks) & (g + dg >= 0) & (g + dg < groups)
        return ok, {"brick": b + db, "group": g + dg}

    def mate(k):
        return {"brick": b, "group": lax.rem(g + k, groups)}

    mates = sorted(range(1, groups), key=lambda k: (abs(2 * k - groups), k))

    expected = 2
    for step in ((1, 0), (-1, 0)):
        ok, peer = reach(step)
        expected = expected + ok.astype(jnp.int32)

        @pl.when(ok)
        def _():
            pl.semaphore_signal(barrier, inc=1, device_id=peer, device_id_type=MESH)

    for k in (1, groups - 1):
        pl.semaphore_signal(barrier, inc=1, device_id=mate(k), device_id_type=MESH)

    hops = [1]
    while 2 ** len(hops) < groups // 2:
        hops.append(2 ** len(hops))

    def tell(i):
        if i < len(hops):
            for k in (hops[i], groups - hops[i]):
                pl.semaphore_signal(word_sem.at[i], inc=1, device_id=mate(k), device_id_type=MESH)

    def hear(i):
        if i < len(hops):
            pl.semaphore_wait(word_sem.at[i], 2)

    loads = [
        pltpu.make_async_copy(ref, x0.at[i, pl.ds(I0, W0), pl.ds(J0, W0), :], load_sem)
        for i, ref in enumerate((f_ref, m_ref, c_ref))
    ]
    for copy in loads:
        copy.start()

    def drain(sem, rows):
        part = tally.at[pl.ds(0, rows)]
        pltpu.make_async_copy(part, part, sem).wait()

    def drain_by_place(sem, rows_of, keep=True):
        wide, deep = (b > 0) & (b < bricks - 1), (g > 0) & (g < groups - 1)
        for nb in (1, 2):
            for ng in (1, 2):
                here = (wide if nb == 2 else ~wide) & (deep if ng == 2 else ~deep)

                @pl.when(here & keep)
                def _():
                    drain(sem, rows_of(nb, ng))

    def blank(rows0, cols0, rows1, cols1):
        shape0, shape1 = (rows0.size, cols0.size, LANES), (rows1.size, cols1.size, LANES)
        for i, value in enumerate((0.0, OUTSIDE_MASS, 0.0)):
            x0[i, rows0, cols0, :] = jnp.full(shape0, value, jnp.float32)
        for i, value in enumerate((OUTSIDE_MASS, 0.0)):
            x1[i, rows1, cols1, :] = jnp.full(shape1, value, jnp.float32)
        f1[rows1, cols1, :] = jnp.zeros(shape1, jnp.float32)

    def blank_patch(v, rows, cols):
        for i, value in enumerate((0.0, OUTSIDE_MASS, 0.0)):
            px[v, i, rows, cols, :] = jnp.full((rows.size, cols.size, LANES), value, jnp.float32)

    def blank_patches(dim, high):
        for v, corner in enumerate(CORNERS):
            if corner[dim] == high:
                rows = pl.ds(5 * high, 5) if dim == 0 else pl.ds(0, 10)
                cols = pl.ds(K0 + 5 * high, 5) if dim == 1 else pl.ds(0, 16)
                blank_patch(v, rows, cols)

    every = (pl.ds(0, E0[0]), pl.ds(0, E0[1]), pl.ds(0, E1[0]), pl.ds(0, E1[1]))

    @pl.when(b == 0)
    def _():
        blank(pl.ds(0, I0), every[1], pl.ds(0, I1), every[3])
        blank_patches(0, 0)

    @pl.when(b == bricks - 1)
    def _():
        blank(pl.ds(I0 + W0, I0), every[1], pl.ds(I1 + H1, I1), every[3])
        blank_patches(0, 1)

    @pl.when(g == 0)
    def _():
        blank(every[0], pl.ds(0, J0), every[2], pl.ds(0, J1))
        blank_patches(1, 0)

    @pl.when(g == groups - 1)
    def _():
        blank(every[0], pl.ds(J0 + W0, J0), every[2], pl.ds(J1 + W1, J1))
        blank_patches(1, 1)

    own0 = (pl.ds(I0, W0), pl.ds(J0, W0))
    drain(load_sem, 3 * W0 * W0)
    own1 = (pl.ds(I1, H1), pl.ds(J1, W1))
    x1[(0, *own1)] = pack_pool(x0[(1, *own0)], pool0)
    x1[(1, *own1)] = pack_pool(x0[(2, *own0)], pool0)

    pl.semaphore_wait(barrier, expected)

    def message(ref, lead, step, widths, at, sizes, send, recv, peer, skip=0):
        si, ti, ni = cut(step[0], at[0], sizes[0], widths[0], skip)
        sj, tj, nj = cut(step[1], at[1], sizes[1], widths[1], 0)
        return pltpu.make_async_remote_copy(
            src_ref=ref.at[(*lead, pl.ds(si, ni), pl.ds(sj, nj))],
            dst_ref=ref.at[(*lead, pl.ds(ti, ni), pl.ds(tj, nj))],
            send_sem=send, recv_sem=recv, device_id=peer, device_id_type=MESH,
        )

    def side_of(step):
        return side_sem.at[step[0] % 3]

    def stage_a(step, peer):
        def part(lead, width):
            return message(
                x0, (lead,), step, (width, width), (I0, J0), (W0, W0), send_sem.at[0], side_of(step), peer
            )

        return [] if step[0] and step[1] else [part(pl.ds(0, 2), 2), part(2, 3)]

    def send_corners(across):
        for ci, cj in CORNERS:
            for di, dj in ((0, 1), (1, 0), (1, 1)):
                if (di and dj) != across:
                    continue
                step = ((2 * ci - 1) * di, (2 * cj - 1) * dj)
                if di and dj:
                    parts = ((pl.ds(0, 2), (0, 4), (0, 4)), (2, (0, 5), (0, 5)))
                elif di:
                    parts = ((pl.ds(0, 2), (2, 2), (0, 3)), (2, (3, 2), (0, 3)))
                else:
                    parts = ((pl.ds(0, 2), (0, 3), (2, 2)), (2, (0, 3), (3, 2)))
                there = CORNERS.index((ci ^ di, cj ^ dj))
                ok, peer = reach(step)

                @pl.when(ok)
                def _():
                    for lead, (ri, ni), (rj, nj) in parts:
                        pi, pj = (5 - ri - ni if ci else ri), (5 - rj - nj if cj else rj)
                        pltpu.make_async_remote_copy(
                            src_ref=x0.at[lead, pl.ds(I0 + 11 * ci + pi, ni), pl.ds(J0 + 11 * cj + pj, nj)],
                            dst_ref=px.at[
                                there, lead, pl.ds(5 * (1 - ci) + pi, ni), pl.ds(K0 + 5 * (1 - cj) + pj, nj)
                            ],
                            send_sem=send_sem.at[4], recv_sem=recv_sem.at[3], device_id=peer, device_id_type=MESH,
                        ).start()

    def stage_b(step, peer):
        def part(lead, widths, skip=0):
            return message(
                x1, (lead,), step, widths, (I1, J1), (H1, W1), send_sem.at[1], recv_sem.at[0], peer, skip
            )

        if step[0] and step[1]:
            return [part(pl.ds(0, 2), (1, 6)), part(pl.ds(0, 2), (2, 4), 1)]
        return [part(0, (3, 0)), part(1, (4, 0))] if step[0] else [part(pl.ds(0, 2), (0, 7))]

    def stage_c(step, peer):
        def part(widths, skip=0):
            return message(f1, (), step, widths, (I1, J1), (H1, W1), send_sem.at[2], recv_sem.at[1], peer, skip)

        return [part((1, 5)), part((2, 3), 1)] if step[0] and step[1] else [part((3, 6))]

    size_a, size_b, size_c = (7 * W0, 7 * W0, 0), (56, 56, 28), (24, 24, 11)
    size_k = (2 * 18, 2 * 18, 57)

    def all_of(size):
        return lambda nb, ng: nb * size[0] + ng * size[1] + nb * ng * size[2]

    def each(stage):
        for step in DIRS:
            ok, peer = reach(step)

            @pl.when(ok)
            def _():
                for copy in stage(step, peer):
                    copy.start()

    tell(0)
    each(stage_a)
    send_corners(0)
    hear(0)
    tell(1)
    send_corners(1)
    each(stage_b)

    block = (x0, inv0, y0, cy0, x20, cx20, base0)

    def diagonal(at, n, fields=block, cols=J8):
        x, inv, y, cy, _, _, _ = fields
        rows = pl.ds(at, n)
        f, m, c = x[0, rows, cols], x[1, rows, cols], x[2, rows, cols]
        invd = inverse(m, c, around_at(x.at[2], at, n, cols))
        first = f * invd
        inv[rows, cols], y[rows, cols], cy[rows, cols] = invd, first, c * first

    def second(at, n, fields=block, cols=J8):
        x, inv, y, cy, x2, cx2, base = fields
        rows = pl.ds(at, n)
        f, c = x[0, rows, cols], x[2, rows, cols]
        s = (0.125 * beta) * (c * around_at(y, at, n, cols) + around_at(cy, at, n, cols))
        fix = inv[rows, cols] * (alpha * f + s)
        x2[rows, cols], cx2[rows, cols], base[rows, cols] = fix, c * fix, (1.0 - alpha) * f - s

    def residual(at, n, fields=block, cols=J8):
        x, _, _, _, x2, cx2, base = fields
        rows = pl.ds(at, n)
        total = x[2, rows, cols] * around_at(x2, at, n, cols) + around_at(cx2, at, n, cols)
        return base[rows, cols] + 0.125 * total

    drain_by_place(side_sem.at[0], lambda nb, ng: ng * size_a[1])
    diagonal(4, 14)
    second(5, 12)
    r0[6:16] = residual(6, 10)
    f1[pl.ds(I1 + 1, 2), pl.ds(J1, W1), :] = pack_pool(r0[7:15], pool0, J0 - 8)
    hear(1)
    tell(2)
    run = 4
    for turn_no in range(2):
        low = (lax.rem(b, run) != 0) if turn_no == 0 else (lax.rem(b, run) == 0)

        def arrived(nb, ng):
            return size_a[0]

        drain_by_place(side_sem.at[1], arrived, low & (b > 0))
        drain_by_place(side_sem.at[2], arrived, ~low & (b < bricks - 1))
        diagonal(jnp.where(low, 1, 18), 3)
        second(jnp.where(low, 2, 17), 3)
        r0[pl.ds(jnp.where(low, 3, 16), 3)] = residual(jnp.where(low, 3, 16), 3)
        quad = pack_pool(r0[pl.ds(jnp.where(low, 3, 15), 4)], pool0, J0 - 8)
        f1[pl.ds(jnp.where(low, I1, I1 + 3), 1), pl.ds(J1, W1), :] = quad
    each(stage_c)
    fine_ref[...] = x20[own0]

    drain_by_place(recv_sem.at[3], all_of(size_k))
    for v, (ci, cj) in enumerate(CORNERS):
        own_i, own_j = 5 * (1 - ci), K0 + 5 * (1 - cj)
        for lead, deep in ((pl.ds(0, 2), 2), (pl.ds(2, 1), 3)):
            for at_i, ni, at_j, nj in ((-deep * (1 - ci), 5 + deep, 0, 5), (0, 5, 5 if cj else -deep, deep)):
                px[v, lead, pl.ds(own_i + at_i, ni), pl.ds(own_j + at_j, nj), :] = x0[
                    lead, pl.ds(I0 + 11 * ci + at_i, ni), pl.ds(J0 + 11 * cj + at_j, nj), :
                ]
        patch = (px.at[v], *(work.at[v, i] for i in range(6)))
        diagonal(1, 8, patch, J4)
        second(2, 6, patch, J4)
        r2 = residual(3, 4, patch, J4)
        pair = halve(jnp.stack([r2[0] + r2[1], r2[2] + r2[3]]), pool3.at[v], 2, 2)
        near[v, 0] = 0.125 * (pair[0] + turn(pair[0], 1))
        near[v, 1] = 0.125 * (pair[1] + turn(pair[1], -1))
        fine_ref[pl.ds(15 * ci, 1), pl.ds(15 * cj, 1), :] = work[v, 3, pl.ds(5 - ci, 1), pl.ds(K0 + 5 - cj, 1), :]

    drain_by_place(recv_sem.at[0], all_of(size_b))
    m1, c1 = x1[0], x1[1]
    c2 = unpack_pool(c1, pool1)
    m2 = unpack_pool(m1, pool1)
    invd1[...] = inverse(m1[1:-1], c1[1:-1], weigh(c1, 2, pairs_beside, w1))
    invd2[...] = inverse(m2[1:-1], c2[1:-1], weigh(c2, 4, rows_beside, w2))
    drain_by_place(send_sem.at[0], all_of(size_a))
    drain_by_place(send_sem.at[1], all_of(size_b))

    drain_by_place(send_sem.at[4], all_of(size_k))
    drain_by_place(send_sem.at[2], all_of(size_c))
    drain_by_place(recv_sem.at[1], all_of(size_c))
    for v, (ci, cj) in enumerate(CORNERS):
        for lower in range(2):
            at = (I1 - 1 + H1 * ci + lower, pl.ds(J1 - 1 + W1 * cj, 2))
            old = f1[at]
            f1[at] = jnp.where(lanes_of(old) % 2 == 1 - lower, near[v, lower], old)
    f = f1[1:-1]
    invd = invd1[...]
    edge = jnp.zeros((1, *E1[1:]), jnp.float32)
    y = jnp.concatenate([edge, f * invd, edge], axis=0)
    s = beta * spread(y, 2, pairs_beside, lambda i: w1[i])
    x2 = invd * (alpha * f + s)
    middle = x2[3:7, J1 : J1 + W1]
    r2 = (1.0 - alpha) * f[1:-1] - s[1:-1] + spread(x2, 2, pairs_beside, lambda i: w1[i, 1:9])

    f = unpack_pool(r2, pool1)
    invd = invd2[1:9]
    s = beta * spread(f * invd, 4, rows_beside, lambda i: w2[i, 2:8])
    x2 = invd[1:-1] * (alpha * f[1:-1] + s)
    coarse = x2[1:5, 4:8]
    r2 = (1.0 - alpha) * f[2:-2] - s[1:-1] + spread(x2, 4, rows_beside, lambda i: w2[i, 3:7])

    pool2[0], pool2[1] = r2[0] + r2[1], r2[2] + r2[3]
    both = pool2[:, pl.ds(4, 2, stride=2), :] + pool2[:, pl.ds(5, 2, stride=2), :]
    upper = both[0] + turn(both[0], -4)
    lower = turn(both[1], 1) + turn(both[1], -3)
    f3[...] = 0.125 * jnp.where(lanes_of(upper) % 2 == 0, upper, lower)

    hear(2)
    for k in mates:
        pltpu.make_async_remote_copy(
            src_ref=f3, dst_ref=gather_ref.at[g], send_sem=send_sem.at[3], recv_sem=recv_sem.at[2],
            device_id=mate(k), device_id_type=MESH,
        ).start()

    gather_ref[g] = f3[...]
    flat = middle.reshape(H1 * W1, LANES)
    for side in range(2):
        rows = squeeze(flat, 2, side).reshape(H1, W1, LANES // 2)
        for i in range(H1):
            middle_ref[2 * i + side] = rows[i]
    for i in range(4):
        coarse_ref[i] = squeeze(coarse[i], 4)

    drain(send_sem.at[3], 2 * (groups - 1))
    drain(recv_sem.at[2], 2 * (groups - 1))


def finish_kernel(fine, middle, coarse, gathered, fine_out, middle_out, coarse_out, rhs_out, rhs, sem):
    copies = [
        pltpu.make_async_copy(source, target, sem.at[i])
        for i, (source, target) in enumerate(((fine, fine_out), (middle, middle_out), (coarse, coarse_out)))
    ]
    for copy in copies:
        copy.start()
    depth = rhs.shape[1]
    row = lax.broadcasted_iota(jnp.int32, (2 * depth, LANES), 0)
    lane = lax.broadcasted_iota(jnp.int32, (2 * depth, LANES), 1)
    pick = lane == 8 * (row % depth) + row // depth
    both = lax.dot_general(
        pick.astype(jnp.float32), gathered[...].reshape(-1, LANES), (((1,), (1,)), ((), ())),
        precision=lax.Precision.HIGHEST, preferred_element_type=jnp.float32,
    )
    rhs[0], rhs[1] = both[:depth], both[depth:]
    last = pltpu.make_async_copy(rhs, rhs_out, sem.at[3])
    last.start()
    for copy in (*copies, last):
        copy.wait()


def solution(mesh):
    bricks, groups = mesh.shape["brick"], mesh.shape["group"]
    anywhere = pl.BlockSpec(memory_space=pl.ANY)
    vmem = pl.BlockSpec(memory_space=pltpu.VMEM)

    def buf(*shape):
        return pltpu.VMEM(shape, jnp.float32)

    dma = pltpu.SemaphoreType.DMA

    def body(right_side, mass_coef, face_coef):
        small = ((W0, W0, LANES), (W1, W1, LANES // 2), (4, 4, LANES // 4))
        held = pl.pallas_call(
            functools.partial(main_kernel, bricks, groups),
            out_shape=(*(buf(*shape) for shape in small), buf(groups, 2, LANES)),
            in_specs=[anywhere] * 3,
            out_specs=(vmem,) * 4,
            scratch_shapes=[
                buf(3, *E0), buf(2, *E1), buf(*E1),
                *([buf(*E0)] * 6), buf(E0[0], 24, LANES),
                buf(2, 4, 24, LANES), buf(12, 24, LANES), buf(2, 12, LANES), buf(2, LANES),
                buf(3 * W0 * W0, LANES),
                buf(6, 10, 24, LANES), buf(6, 10, 12, LANES), buf(10, 24, LANES), buf(10, 12, LANES),
                buf(4, 3, *PATCH), buf(4, 6, *PATCH), buf(4, 2, 8, LANES), buf(4, 2, 2, LANES),
                dma, dma((5,)), dma((3,)), dma((4,)), pltpu.SemaphoreType.REGULAR((3,)),
            ],
            compiler_params=pltpu.CompilerParams(collective_id=0, has_side_effects=True),
            name="cycle",
        )(right_side, mass_coef, face_coef)
        held = [pltpu.with_memory_space_constraint(array, pltpu.VMEM) for array in held]
        rhs_shape = (2, LANES // 8, 2 * groups)
        fine, middle, coarse, rhs = pl.pallas_call(
            finish_kernel,
            out_shape=tuple(jax.ShapeDtypeStruct(shape, jnp.float32) for shape in (*small, rhs_shape)),
            in_specs=[vmem] * 4,
            out_specs=(anywhere,) * 4,
            scratch_shapes=[buf(*rhs_shape), dma((4,))],
            name="finish",
        )(*held)
        return fine, middle, coarse, jnp.swapaxes(rhs, 1, 2)

    placed = P("brick", "group", None)
    return jax.shard_map(
        body,
        mesh=mesh,
        in_specs=(placed, placed, placed),
        out_specs=(placed, placed, placed, P("brick", None, None)),
        check_vma=False,
    )
```

```python
import functools

import jax
import jax.numpy as jnp
from jax import lax
from jax.experimental import pallas as pl
from jax.experimental.pallas import tpu as pltpu
from jax.sharding import PartitionSpec as P

MESH = pl.DeviceIdType.MESH

center_value = 1.1
half_width = 0.8
ratio_sigma = center_value / half_width
first_rho = 1.0 / ratio_sigma
second_rho = 1.0 / (2.0 * ratio_sigma - first_rho)
carry_factor = second_rho * first_rho
push_factor = 2.0 * second_rho / half_width

alpha = (1.0 + carry_factor) / center_value + push_factor * (1.0 - 1.0 / center_value)
beta = push_factor / center_value

OUTSIDE_MASS = 1e30
LANES = 128
I0, J0, W0, E0 = 3, 12, 16, (22, 40, LANES)
J8 = pl.ds(8, 24)
K0, PATCH = 3, (10, 16, LANES)
J4 = pl.ds(4, 8)
CORNERS = [(1, 1), (1, 0), (0, 1), (0, 0)]
I1, H1, J1, W1, E1 = 4, 4, 8, 8, (12, 24, LANES)

DIRS = [(1, 1), (1, -1), (-1, 1), (-1, -1), (1, 0), (-1, 0), (0, 1), (0, -1)]


def cut(step, start, size, width, skip):
    if step == 0:
        return start, start, size
    if step > 0:
        return start + size - width - skip, start - width - skip, width
    return start + skip, start + size + skip, width


def lanes_of(a):
    return lax.broadcasted_iota(jnp.int32, a.shape, a.ndim - 1)


def turn(a, by):
    return pltpu.roll(a, by % LANES, axis=a.ndim - 1)


def beside(mid, by):
    lane = lanes_of(mid)
    low = jnp.where(lane >= by, turn(mid, by), 0.0)
    high = jnp.where(lane < LANES - by, turn(mid, -by), 0.0)
    cols = mid.shape[1]
    return low + high + pltpu.roll(mid, 1, axis=1) + pltpu.roll(mid, cols - 1, axis=1)


def around_at(ref, at, n, cols):
    rows = pl.ds(at, n)
    mid = ref[rows, cols]
    lane = lanes_of(mid)
    low, high = jnp.where(lane >= 1, turn(mid, 1), 0.0), jnp.where(lane < LANES - 1, turn(mid, -1), 0.0)
    left, right = pl.ds(cols.start - 1, cols.size), pl.ds(cols.start + 1, cols.size)
    return ref[pl.ds(at - 1, n), cols] + ref[pl.ds(at + 1, n), cols] + (ref[rows, left] + ref[rows, right]) + (low + high)


def around(a, by):
    return a[2:] + a[:-2] + beside(a[1:-1], by)


def rows_beside(a):
    return a[:-2], a[2:]


def pairs_beside(a):
    up, down = turn(a[:-1], -1), turn(a[1:], 1)
    even = lanes_of(a[1:-1]) % 2 == 0
    return jnp.where(even, up[:-1], down[:-1]), jnp.where(even, up[1:], down[1:])


def six(a, by, rows):
    mid = a[1:-1]
    return (
        *rows(a), pltpu.roll(mid, 1, axis=1), pltpu.roll(mid, mid.shape[1] - 1, axis=1), turn(mid, by), turn(mid, -by)
    )


def weigh(c, by, rows, out):
    mid = c[1:-1]
    lane = lanes_of(mid)
    total = None
    for i, near in enumerate(six(c, by, rows)):
        inside = {4: lane >= by, 5: lane < LANES - by}.get(i)
        if inside is not None:
            near = jnp.where(inside, near, 0.0)
        weight = 0.125 * (mid + near)
        out[i] = weight if inside is None else jnp.where(inside, weight, 0.0)
        total = near if total is None else total + near
    return total


def spread(u, by, rows, weights):
    near = six(u, by, rows)
    parts = [weights(i) * near[i] for i in range(6)]
    return ((parts[0] + parts[1]) + (parts[2] + parts[3])) + (parts[4] + parts[5])


def inverse(m, c, total):
    diag = m + 0.75 * c + 0.125 * total
    rough = pl.reciprocal(diag, approx=True)
    rough = rough * (2.0 - diag * rough)
    return rough * (2.0 - diag * rough)


def squeeze(a, by, first=0):
    shape = (LANES, LANES // by)
    pick = lax.broadcasted_iota(jnp.int32, shape, 0) == by * lax.broadcasted_iota(jnp.int32, shape, 1) + first
    return lax.dot(
        a, pick.astype(jnp.float32), precision=lax.Precision.HIGHEST, preferred_element_type=jnp.float32
    )


def halve(a, scratch, first=0, count=None):
    rows, cols, _ = a.shape
    count = count or cols // 2
    scratch[0:rows, 0:cols, :] = a
    even, odd = pl.ds(first, count, stride=2), pl.ds(first + 1, count, stride=2)
    return scratch[0:rows, even, :] + scratch[0:rows, odd, :]


def pack_pool(a, scratch, first=0):
    rows, cols, _ = a.shape
    quad = a.reshape(rows // 4, 4, cols, LANES)
    upper = halve(quad[:, 0] + quad[:, 1], scratch.at[0], first, W1)
    lower = halve(quad[:, 2] + quad[:, 3], scratch.at[1], first, W1)
    even = lanes_of(upper) % 2 == 0
    return 0.125 * jnp.where(even, upper + turn(upper, -1), lower + turn(lower, 1))


def unpack_pool(a, scratch):
    both = halve(a, scratch)
    both = both + turn(both, -1)
    return 0.125 * (both + turn(both, -2))


def main_kernel(
    bricks, groups,
    f_ref, m_ref, c_ref,
    fine_ref, middle_ref, coarse_ref, gather_ref,
    x0, x1, f1, inv0, y0, cy0, x20, cx20, base0, r0, pool0, pool1, pool2, f3, tally, w1, w2, invd1, invd2, px, work, pool3, near,
    load_sem, send_sem, side_sem, recv_sem, word_sem,
):
    b, g = lax.axis_index("brick"), lax.axis_index("group")
    barrier = pltpu.get_barrier_semaphore()

    def reach(step):
        db, dg = step
        ok = (b + db >= 0) & (b + db < bricks) & (g + dg >= 0) & (g + dg < groups)
        return ok, {"brick": b + db, "group": g + dg}

    def mate(k):
        return {"brick": b, "group": lax.rem(g + k, groups)}

    mates = sorted(range(1, groups), key=lambda k: (abs(2 * k - groups), k))

    expected = 2
    for step in ((1, 0), (-1, 0)):
        ok, peer = reach(step)
        expected = expected + ok.astype(jnp.int32)

        @pl.when(ok)
        def _():
            pl.semaphore_signal(barrier, inc=1, device_id=peer, device_id_type=MESH)

    for k in (1, groups - 1):
        pl.semaphore_signal(barrier, inc=1, device_id=mate(k), device_id_type=MESH)

    hops = [1]
    while 2 ** len(hops) < groups // 2:
        hops.append(2 ** len(hops))

    def tell(i):
        if i < len(hops):
            for k in (hops[i], groups - hops[i]):
                pl.semaphore_signal(word_sem.at[i], inc=1, device_id=mate(k), device_id_type=MESH)

    def hear(i):
        if i < len(hops):
            pl.semaphore_wait(word_sem.at[i], 2)

    loads = [
        pltpu.make_async_copy(ref, x0.at[i, pl.ds(I0, W0), pl.ds(J0, W0), :], load_sem)
        for i, ref in enumerate((f_ref, m_ref, c_ref))
    ]
    for copy in loads:
        copy.start()

    def drain(sem, rows):
        part = tally.at[pl.ds(0, rows)]
        pltpu.make_async_copy(part, part, sem).wait()

    def drain_by_place(sem, rows_of, keep=True):
        wide, deep = (b > 0) & (b < bricks - 1), (g > 0) & (g < groups - 1)
        for nb in (1, 2):
            for ng in (1, 2):
                here = (wide if nb == 2 else ~wide) & (deep if ng == 2 else ~deep)

                @pl.when(here & keep)
                def _():
                    drain(sem, rows_of(nb, ng))

    def blank(rows0, cols0, rows1, cols1):
        shape0, shape1 = (rows0.size, cols0.size, LANES), (rows1.size, cols1.size, LANES)
        for i, value in enumerate((0.0, OUTSIDE_MASS, 0.0)):
            x0[i, rows0, cols0, :] = jnp.full(shape0, value, jnp.float32)
        for i, value in enumerate((OUTSIDE_MASS, 0.0)):
            x1[i, rows1, cols1, :] = jnp.full(shape1, value, jnp.float32)
        f1[rows1, cols1, :] = jnp.zeros(shape1, jnp.float32)

    def blank_patch(v, rows, cols):
        for i, value in enumerate((0.0, OUTSIDE_MASS, 0.0)):
            px[v, i, rows, cols, :] = jnp.full((rows.size, cols.size, LANES), value, jnp.float32)

    def blank_patches(dim, high):
        for v, corner in enumerate(CORNERS):
            if corner[dim] == high:
                rows = pl.ds(5 * high, 5) if dim == 0 else pl.ds(0, 10)
                cols = pl.ds(K0 + 5 * high, 5) if dim == 1 else pl.ds(0, 16)
                blank_patch(v, rows, cols)

    every = (pl.ds(0, E0[0]), pl.ds(0, E0[1]), pl.ds(0, E1[0]), pl.ds(0, E1[1]))

    @pl.when(b == 0)
    def _():
        blank(pl.ds(0, I0), every[1], pl.ds(0, I1), every[3])
        blank_patches(0, 0)

    @pl.when(b == bricks - 1)
    def _():
        blank(pl.ds(I0 + W0, I0), every[1], pl.ds(I1 + H1, I1), every[3])
        blank_patches(0, 1)

    @pl.when(g == 0)
    def _():
        blank(every[0], pl.ds(0, J0), every[2], pl.ds(0, J1))
        blank_patches(1, 0)

    @pl.when(g == groups - 1)
    def _():
        blank(every[0], pl.ds(J0 + W0, J0), every[2], pl.ds(J1 + W1, J1))
        blank_patches(1, 1)

    own0 = (pl.ds(I0, W0), pl.ds(J0, W0))
    drain(load_sem, 3 * W0 * W0)
    own1 = (pl.ds(I1, H1), pl.ds(J1, W1))
    x1[(0, *own1)] = pack_pool(x0[(1, *own0)], pool0)
    x1[(1, *own1)] = pack_pool(x0[(2, *own0)], pool0)

    pl.semaphore_wait(barrier, expected)

    def message(ref, lead, step, widths, at, sizes, send, recv, peer, skip=0):
        si, ti, ni = cut(step[0], at[0], sizes[0], widths[0], skip)
        sj, tj, nj = cut(step[1], at[1], sizes[1], widths[1], 0)
        return pltpu.make_async_remote_copy(
            src_ref=ref.at[(*lead, pl.ds(si, ni), pl.ds(sj, nj))],
            dst_ref=ref.at[(*lead, pl.ds(ti, ni), pl.ds(tj, nj))],
            send_sem=send, recv_sem=recv, device_id=peer, device_id_type=MESH,
        )

    def side_of(step):
        return side_sem.at[step[0] % 3]

    def stage_a(step, peer):
        def part(lead, width):
            return message(
                x0, (lead,), step, (width, width), (I0, J0), (W0, W0), send_sem.at[0], side_of(step), peer
            )

        return [] if step[0] and step[1] else [part(pl.ds(0, 2), 2), part(2, 3)]

    def send_corners(across):
        for ci, cj in CORNERS:
            for di, dj in ((0, 1), (1, 0), (1, 1)):
                if (di and dj) != across:
                    continue
                step = ((2 * ci - 1) * di, (2 * cj - 1) * dj)
                if di and dj:
                    parts = ((pl.ds(0, 2), (0, 4), (0, 4)), (2, (0, 5), (0, 5)))
                elif di:
                    parts = ((pl.ds(0, 2), (2, 2), (0, 3)), (2, (3, 2), (0, 3)))
                else:
                    parts = ((pl.ds(0, 2), (0, 3), (2, 2)), (2, (0, 3), (3, 2)))
                there = CORNERS.index((ci ^ di, cj ^ dj))
                ok, peer = reach(step)

                @pl.when(ok)
                def _():
                    for lead, (ri, ni), (rj, nj) in parts:
                        pi, pj = (5 - ri - ni if ci else ri), (5 - rj - nj if cj else rj)
                        pltpu.make_async_remote_copy(
                            src_ref=x0.at[lead, pl.ds(I0 + 11 * ci + pi, ni), pl.ds(J0 + 11 * cj + pj, nj)],
                            dst_ref=px.at[
                                there, lead, pl.ds(5 * (1 - ci) + pi, ni), pl.ds(K0 + 5 * (1 - cj) + pj, nj)
                            ],
                            send_sem=send_sem.at[4], recv_sem=recv_sem.at[3], device_id=peer, device_id_type=MESH,
                        ).start()

    def stage_b(step, peer):
        def part(lead, widths, skip=0):
            return message(
                x1, (lead,), step, widths, (I1, J1), (H1, W1), send_sem.at[1], recv_sem.at[0], peer, skip
            )

        if step[0] and step[1]:
            return [part(pl.ds(0, 2), (1, 6)), part(pl.ds(0, 2), (2, 4), 1)]
        return [part(0, (3, 0)), part(1, (4, 0))] if step[0] else [part(pl.ds(0, 2), (0, 7))]

    def stage_c(step, peer):
        def part(widths, skip=0):
            return message(f1, (), step, widths, (I1, J1), (H1, W1), send_sem.at[2], recv_sem.at[1], peer, skip)

        return [part((1, 5)), part((2, 3), 1)] if step[0] and step[1] else [part((3, 6))]

    size_a, size_b, size_c = (7 * W0, 7 * W0, 0), (56, 56, 28), (24, 24, 11)
    size_k = (2 * 18, 2 * 18, 57)

    def all_of(size):
        return lambda nb, ng: nb * size[0] + ng * size[1] + nb * ng * size[2]

    def each(stage):
        for step in DIRS:
            ok, peer = reach(step)

            @pl.when(ok)
            def _():
                for copy in stage(step, peer):
                    copy.start()

    tell(0)
    each(stage_a)
    send_corners(0)
    hear(0)
    tell(1)

    block = (x0, inv0, y0, cy0, x20, cx20, base0)

    def diagonal(at, n, fields=block, cols=J8):
        x, inv, y, cy, _, _, _ = fields
        rows = pl.ds(at, n)
        f, m, c = x[0, rows, cols], x[1, rows, cols], x[2, rows, cols]
        invd = inverse(m, c, around_at(x.at[2], at, n, cols))
        first = f * invd
        inv[rows, cols], y[rows, cols], cy[rows, cols] = invd, first, c * first

    def second(at, n, fields=block, cols=J8):
        x, inv, y, cy, x2, cx2, base = fields
        rows = pl.ds(at, n)
        f, c = x[0, rows, cols], x[2, rows, cols]
        s = (0.125 * beta) * (c * around_at(y, at, n, cols) + around_at(cy, at, n, cols))
        fix = inv[rows, cols] * (alpha * f + s)
        x2[rows, cols], cx2[rows, cols], base[rows, cols] = fix, c * fix, (1.0 - alpha) * f - s

    def residual(at, n, fields=block, cols=J8):
        x, _, _, _, x2, cx2, base = fields
        rows = pl.ds(at, n)
        total = x[2, rows, cols] * around_at(x2, at, n, cols) + around_at(cx2, at, n, cols)
        return base[rows, cols] + 0.125 * total

    drain_by_place(side_sem.at[0], lambda nb, ng: ng * size_a[1])
    send_corners(1)
    each(stage_b)
    diagonal(4, 14)
    second(5, 12)
    r0[6:16] = residual(6, 10)
    f1[pl.ds(I1 + 1, 2), pl.ds(J1, W1), :] = pack_pool(r0[7:15], pool0, J0 - 8)
    hear(1)
    tell(2)
    run = 4
    for turn_no in range(2):
        low = (lax.rem(b, run) != 0) if turn_no == 0 else (lax.rem(b, run) == 0)

        def arrived(nb, ng):
            return size_a[0]

        drain_by_place(side_sem.at[1], arrived, low & (b > 0))
        drain_by_place(side_sem.at[2], arrived, ~low & (b < bricks - 1))
        diagonal(jnp.where(low, 1, 18), 3)
        second(jnp.where(low, 2, 17), 3)
        r0[pl.ds(jnp.where(low, 3, 16), 3)] = residual(jnp.where(low, 3, 16), 3)
        quad = pack_pool(r0[pl.ds(jnp.where(low, 3, 15), 4)], pool0, J0 - 8)
        f1[pl.ds(jnp.where(low, I1, I1 + 3), 1), pl.ds(J1, W1), :] = quad
    each(stage_c)
    fine_ref[...] = x20[own0]

    drain_by_place(recv_sem.at[3], all_of(size_k))
    for v, (ci, cj) in enumerate(CORNERS):
        own_i, own_j = 5 * (1 - ci), K0 + 5 * (1 - cj)
        for lead, deep in ((pl.ds(0, 2), 2), (pl.ds(2, 1), 3)):
            for at_i, ni, at_j, nj in ((-deep * (1 - ci), 5 + deep, 0, 5), (0, 5, 5 if cj else -deep, deep)):
                px[v, lead, pl.ds(own_i + at_i, ni), pl.ds(own_j + at_j, nj), :] = x0[
                    lead, pl.ds(I0 + 11 * ci + at_i, ni), pl.ds(J0 + 11 * cj + at_j, nj), :
                ]
        patch = (px.at[v], *(work.at[v, i] for i in range(6)))
        diagonal(1, 8, patch, J4)
        second(2, 6, patch, J4)
        r2 = residual(3, 4, patch, J4)
        pair = halve(jnp.stack([r2[0] + r2[1], r2[2] + r2[3]]), pool3.at[v], 2, 2)
        near[v, 0] = 0.125 * (pair[0] + turn(pair[0], 1))
        near[v, 1] = 0.125 * (pair[1] + turn(pair[1], -1))
        fine_ref[pl.ds(15 * ci, 1), pl.ds(15 * cj, 1), :] = work[v, 3, pl.ds(5 - ci, 1), pl.ds(K0 + 5 - cj, 1), :]

    drain_by_place(recv_sem.at[0], all_of(size_b))
    m1, c1 = x1[0], x1[1]
    c2 = unpack_pool(c1, pool1)
    m2 = unpack_pool(m1, pool1)
    invd1[...] = inverse(m1[1:-1], c1[1:-1], weigh(c1, 2, pairs_beside, w1))
    invd2[...] = inverse(m2[1:-1], c2[1:-1], weigh(c2, 4, rows_beside, w2))
    drain_by_place(send_sem.at[0], all_of(size_a))
    drain_by_place(send_sem.at[1], all_of(size_b))

    drain_by_place(send_sem.at[4], all_of(size_k))
    drain_by_place(send_sem.at[2], all_of(size_c))
    drain_by_place(recv_sem.at[1], all_of(size_c))
    for v, (ci, cj) in enumerate(CORNERS):
        for lower in range(2):
            at = (I1 - 1 + H1 * ci + lower, pl.ds(J1 - 1 + W1 * cj, 2))
            old = f1[at]
            f1[at] = jnp.where(lanes_of(old) % 2 == 1 - lower, near[v, lower], old)
    f = f1[1:-1]
    invd = invd1[...]
    edge = jnp.zeros((1, *E1[1:]), jnp.float32)
    y = jnp.concatenate([edge, f * invd, edge], axis=0)
    s = beta * spread(y, 2, pairs_beside, lambda i: w1[i])
    x2 = invd * (alpha * f + s)
    middle = x2[3:7, J1 : J1 + W1]
    r2 = (1.0 - alpha) * f[1:-1] - s[1:-1] + spread(x2, 2, pairs_beside, lambda i: w1[i, 1:9])

    f = unpack_pool(r2, pool1)
    invd = invd2[1:9]
    s = beta * spread(f * invd, 4, rows_beside, lambda i: w2[i, 2:8])
    x2 = invd[1:-1] * (alpha * f[1:-1] + s)
    coarse = x2[1:5, 4:8]
    r2 = (1.0 - alpha) * f[2:-2] - s[1:-1] + spread(x2, 4, rows_beside, lambda i: w2[i, 3:7])

    pool2[0], pool2[1] = r2[0] + r2[1], r2[2] + r2[3]
    both = pool2[:, pl.ds(4, 2, stride=2), :] + pool2[:, pl.ds(5, 2, stride=2), :]
    upper = both[0] + turn(both[0], -4)
    lower = turn(both[1], 1) + turn(both[1], -3)
    f3[...] = 0.125 * jnp.where(lanes_of(upper) % 2 == 0, upper, lower)

    hear(2)
    for k in mates:
        pltpu.make_async_remote_copy(
            src_ref=f3, dst_ref=gather_ref.at[g], send_sem=send_sem.at[3], recv_sem=recv_sem.at[2],
            device_id=mate(k), device_id_type=MESH,
        ).start()

    gather_ref[g] = f3[...]
    flat = middle.reshape(H1 * W1, LANES)
    for side in range(2):
        rows = squeeze(flat, 2, side).reshape(H1, W1, LANES // 2)
        for i in range(H1):
            middle_ref[2 * i + side] = rows[i]
    for i in range(4):
        coarse_ref[i] = squeeze(coarse[i], 4)

    drain(send_sem.at[3], 2 * (groups - 1))
    drain(recv_sem.at[2], 2 * (groups - 1))


def finish_kernel(fine, middle, coarse, gathered, fine_out, middle_out, coarse_out, rhs_out, rhs, sem):
    copies = [
        pltpu.make_async_copy(source, target, sem.at[i])
        for i, (source, target) in enumerate(((fine, fine_out), (middle, middle_out), (coarse, coarse_out)))
    ]
    for copy in copies:
        copy.start()
    depth = rhs.shape[1]
    row = lax.broadcasted_iota(jnp.int32, (2 * depth, LANES), 0)
    lane = lax.broadcasted_iota(jnp.int32, (2 * depth, LANES), 1)
    pick = lane == 8 * (row % depth) + row // depth
    both = lax.dot_general(
        pick.astype(jnp.float32), gathered[...].reshape(-1, LANES), (((1,), (1,)), ((), ())),
        precision=lax.Precision.HIGHEST, preferred_element_type=jnp.float32,
    )
    rhs[0], rhs[1] = both[:depth], both[depth:]
    last = pltpu.make_async_copy(rhs, rhs_out, sem.at[3])
    last.start()
    for copy in (*copies, last):
        copy.wait()


def solution(mesh):
    bricks, groups = mesh.shape["brick"], mesh.shape["group"]
    anywhere = pl.BlockSpec(memory_space=pl.ANY)
    vmem = pl.BlockSpec(memory_space=pltpu.VMEM)

    def buf(*shape):
        return pltpu.VMEM(shape, jnp.float32)

    dma = pltpu.SemaphoreType.DMA

    def body(right_side, mass_coef, face_coef):
        small = ((W0, W0, LANES), (W1, W1, LANES // 2), (4, 4, LANES // 4))
        held = pl.pallas_call(
            functools.partial(main_kernel, bricks, groups),
            out_shape=(*(buf(*shape) for shape in small), buf(groups, 2, LANES)),
            in_specs=[anywhere] * 3,
            out_specs=(vmem,) * 4,
            scratch_shapes=[
                buf(3, *E0), buf(2, *E1), buf(*E1),
                *([buf(*E0)] * 6), buf(E0[0], 24, LANES),
                buf(2, 4, 24, LANES), buf(12, 24, LANES), buf(2, 12, LANES), buf(2, LANES),
                buf(3 * W0 * W0, LANES),
                buf(6, 10, 24, LANES), buf(6, 10, 12, LANES), buf(10, 24, LANES), buf(10, 12, LANES),
                buf(4, 3, *PATCH), buf(4, 6, *PATCH), buf(4, 2, 8, LANES), buf(4, 2, 2, LANES),
                dma, dma((5,)), dma((3,)), dma((4,)), pltpu.SemaphoreType.REGULAR((3,)),
            ],
            compiler_params=pltpu.CompilerParams(collective_id=0, has_side_effects=True),
            name="cycle",
        )(right_side, mass_coef, face_coef)
        held = [pltpu.with_memory_space_constraint(array, pltpu.VMEM) for array in held]
        rhs_shape = (2, LANES // 8, 2 * groups)
        fine, middle, coarse, rhs = pl.pallas_call(
            finish_kernel,
            out_shape=tuple(jax.ShapeDtypeStruct(shape, jnp.float32) for shape in (*small, rhs_shape)),
            in_specs=[vmem] * 4,
            out_specs=(anywhere,) * 4,
            scratch_shapes=[buf(*rhs_shape), dma((4,))],
            name="finish",
        )(*held)
        return fine, middle, coarse, jnp.swapaxes(rhs, 1, 2)

    placed = P("brick", "group", None)
    return jax.shard_map(
        body,
        mesh=mesh,
        in_specs=(placed, placed, placed),
        out_specs=(placed, placed, placed, P("brick", None, None)),
        check_vma=False,
    )
```

```python
import functools

import jax
import jax.numpy as jnp
from jax import lax
from jax.experimental import pallas as pl
from jax.experimental.pallas import tpu as pltpu
from jax.sharding import PartitionSpec as P

MESH = pl.DeviceIdType.MESH

center_value = 1.1
half_width = 0.8
ratio_sigma = center_value / half_width
first_rho = 1.0 / ratio_sigma
second_rho = 1.0 / (2.0 * ratio_sigma - first_rho)
carry_factor = second_rho * first_rho
push_factor = 2.0 * second_rho / half_width

alpha = (1.0 + carry_factor) / center_value + push_factor * (1.0 - 1.0 / center_value)
beta = push_factor / center_value

OUTSIDE_MASS = 1e30
LANES = 128
I0, J0, W0, E0 = 3, 12, 16, (22, 40, LANES)
J8 = pl.ds(8, 24)
K0, PATCH = 3, (10, 16, LANES)
J4 = pl.ds(4, 8)
CORNERS = [(1, 1), (1, 0), (0, 1), (0, 0)]
I1, H1, J1, W1, E1 = 4, 4, 8, 8, (12, 24, LANES)

DIRS = [(1, 1), (1, -1), (-1, 1), (-1, -1), (1, 0), (-1, 0), (0, 1), (0, -1)]


def cut(step, start, size, width, skip):
    if step == 0:
        return start, start, size
    if step > 0:
        return start + size - width - skip, start - width - skip, width
    return start + skip, start + size + skip, width


def lanes_of(a):
    return lax.broadcasted_iota(jnp.int32, a.shape, a.ndim - 1)


def turn(a, by):
    return pltpu.roll(a, by % LANES, axis=a.ndim - 1)


def beside(mid, by):
    lane = lanes_of(mid)
    low = jnp.where(lane >= by, turn(mid, by), 0.0)
    high = jnp.where(lane < LANES - by, turn(mid, -by), 0.0)
    cols = mid.shape[1]
    return low + high + pltpu.roll(mid, 1, axis=1) + pltpu.roll(mid, cols - 1, axis=1)


def around_at(ref, at, n, cols):
    rows = pl.ds(at, n)
    mid = ref[rows, cols]
    lane = lanes_of(mid)
    low, high = jnp.where(lane >= 1, turn(mid, 1), 0.0), jnp.where(lane < LANES - 1, turn(mid, -1), 0.0)
    left, right = pl.ds(cols.start - 1, cols.size), pl.ds(cols.start + 1, cols.size)
    return ref[pl.ds(at - 1, n), cols] + ref[pl.ds(at + 1, n), cols] + (ref[rows, left] + ref[rows, right]) + (low + high)


def around(a, by):
    return a[2:] + a[:-2] + beside(a[1:-1], by)


def rows_beside(a):
    return a[:-2], a[2:]


def pairs_beside(a):
    up, down = turn(a[:-1], -1), turn(a[1:], 1)
    even = lanes_of(a[1:-1]) % 2 == 0
    return jnp.where(even, up[:-1], down[:-1]), jnp.where(even, up[1:], down[1:])


def six(a, by, rows):
    mid = a[1:-1]
    return (
        *rows(a), pltpu.roll(mid, 1, axis=1), pltpu.roll(mid, mid.shape[1] - 1, axis=1), turn(mid, by), turn(mid, -by)
    )


def weigh(c, by, rows, out):
    mid = c[1:-1]
    lane = lanes_of(mid)
    total = None
    for i, near in enumerate(six(c, by, rows)):
        inside = {4: lane >= by, 5: lane < LANES - by}.get(i)
        if inside is not None:
            near = jnp.where(inside, near, 0.0)
        weight = 0.125 * (mid + near)
        out[i] = weight if inside is None else jnp.where(inside, weight, 0.0)
        total = near if total is None else total + near
    return total


def spread(u, by, rows, weights):
    near = six(u, by, rows)
    parts = [weights(i) * near[i] for i in range(6)]
    return ((parts[0] + parts[1]) + (parts[2] + parts[3])) + (parts[4] + parts[5])


def inverse(m, c, total):
    diag = m + 0.75 * c + 0.125 * total
    rough = pl.reciprocal(diag, approx=True)
    rough = rough * (2.0 - diag * rough)
    return rough * (2.0 - diag * rough)


def squeeze(a, by, first=0):
    shape = (LANES, LANES // by)
    pick = lax.broadcasted_iota(jnp.int32, shape, 0) == by * lax.broadcasted_iota(jnp.int32, shape, 1) + first
    return lax.dot(
        a, pick.astype(jnp.float32), precision=lax.Precision.HIGHEST, preferred_element_type=jnp.float32
    )


def halve(a, scratch, first=0, count=None):
    rows, cols, _ = a.shape
    count = count or cols // 2
    scratch[0:rows, 0:cols, :] = a
    even, odd = pl.ds(first, count, stride=2), pl.ds(first + 1, count, stride=2)
    return scratch[0:rows, even, :] + scratch[0:rows, odd, :]


def pack_pool(a, scratch, first=0):
    rows, cols, _ = a.shape
    quad = a.reshape(rows // 4, 4, cols, LANES)
    upper = halve(quad[:, 0] + quad[:, 1], scratch.at[0], first, W1)
    lower = halve(quad[:, 2] + quad[:, 3], scratch.at[1], first, W1)
    even = lanes_of(upper) % 2 == 0
    return 0.125 * jnp.where(even, upper + turn(upper, -1), lower + turn(lower, 1))


def unpack_pool(a, scratch):
    both = halve(a, scratch)
    both = both + turn(both, -1)
    return 0.125 * (both + turn(both, -2))


def main_kernel(
    bricks, groups,
    f_ref, m_ref, c_ref,
    fine_ref, middle_ref, coarse_ref, gather_ref,
    x0, x1, f1, inv0, y0, cy0, x20, cx20, base0, r0, pool0, pool1, pool2, f3, tally, w1, w2, invd1, invd2, px, work, pool3, near,
    load_sem, send_sem, side_sem, recv_sem, word_sem,
):
    b, g = lax.axis_index("brick"), lax.axis_index("group")
    barrier = pltpu.get_barrier_semaphore()

    def reach(step):
        db, dg = step
        ok = (b + db >= 0) & (b + db < bricks) & (g + dg >= 0) & (g + dg < groups)
        return ok, {"brick": b + db, "group": g + dg}

    def mate(k):
        return {"brick": b, "group": lax.rem(g + k, groups)}

    mates = sorted(range(1, groups), key=lambda k: (abs(2 * k - groups), k))

    expected = 2
    for step in ((1, 0), (-1, 0)):
        ok, peer = reach(step)
        expected = expected + ok.astype(jnp.int32)

        @pl.when(ok)
        def _():
            pl.semaphore_signal(barrier, inc=1, device_id=peer, device_id_type=MESH)

    for k in (1, groups - 1):
        pl.semaphore_signal(barrier, inc=1, device_id=mate(k), device_id_type=MESH)

    hops = [1]
    while 2 ** len(hops) < groups // 2:
        hops.append(2 ** len(hops))

    def tell(i):
        if i < len(hops):
            for k in (hops[i], groups - hops[i]):
                pl.semaphore_signal(word_sem.at[i], inc=1, device_id=mate(k), device_id_type=MESH)

    def hear(i):
        if i < len(hops):
            pl.semaphore_wait(word_sem.at[i], 2)

    loads = [
        pltpu.make_async_copy(ref, x0.at[i, pl.ds(I0, W0), pl.ds(J0, W0), :], load_sem)
        for i, ref in enumerate((f_ref, m_ref, c_ref))
    ]
    for copy in loads:
        copy.start()

    def drain(sem, rows):
        part = tally.at[pl.ds(0, rows)]
        pltpu.make_async_copy(part, part, sem).wait()

    def drain_by_place(sem, rows_of, keep=True):
        wide, deep = (b > 0) & (b < bricks - 1), (g > 0) & (g < groups - 1)
        for nb in (1, 2):
            for ng in (1, 2):
                here = (wide if nb == 2 else ~wide) & (deep if ng == 2 else ~deep)

                @pl.when(here & keep)
                def _():
                    drain(sem, rows_of(nb, ng))

    def blank(rows0, cols0, rows1, cols1):
        shape0, shape1 = (rows0.size, cols0.size, LANES), (rows1.size, cols1.size, LANES)
        for i, value in enumerate((0.0, OUTSIDE_MASS, 0.0)):
            x0[i, rows0, cols0, :] = jnp.full(shape0, value, jnp.float32)
        for i, value in enumerate((OUTSIDE_MASS, 0.0)):
            x1[i, rows1, cols1, :] = jnp.full(shape1, value, jnp.float32)
        f1[rows1, cols1, :] = jnp.zeros(shape1, jnp.float32)

    def blank_patch(v, rows, cols):
        for i, value in enumerate((0.0, OUTSIDE_MASS, 0.0)):
            px[v, i, rows, cols, :] = jnp.full((rows.size, cols.size, LANES), value, jnp.float32)

    def blank_patches(dim, high):
        for v, corner in enumerate(CORNERS):
            if corner[dim] == high:
                rows = pl.ds(5 * high, 5) if dim == 0 else pl.ds(0, 10)
                cols = pl.ds(K0 + 5 * high, 5) if dim == 1 else pl.ds(0, 16)
                blank_patch(v, rows, cols)

    every = (pl.ds(0, E0[0]), pl.ds(0, E0[1]), pl.ds(0, E1[0]), pl.ds(0, E1[1]))

    @pl.when(b == 0)
    def _():
        blank(pl.ds(0, I0), every[1], pl.ds(0, I1), every[3])
        blank_patches(0, 0)

    @pl.when(b == bricks - 1)
    def _():
        blank(pl.ds(I0 + W0, I0), every[1], pl.ds(I1 + H1, I1), every[3])
        blank_patches(0, 1)

    @pl.when(g == 0)
    def _():
        blank(every[0], pl.ds(0, J0), every[2], pl.ds(0, J1))
        blank_patches(1, 0)

    @pl.when(g == groups - 1)
    def _():
        blank(every[0], pl.ds(J0 + W0, J0), every[2], pl.ds(J1 + W1, J1))
        blank_patches(1, 1)

    own0 = (pl.ds(I0, W0), pl.ds(J0, W0))
    drain(load_sem, 3 * W0 * W0)
    own1 = (pl.ds(I1, H1), pl.ds(J1, W1))

    pl.semaphore_wait(barrier, expected)

    def message(ref, lead, step, widths, at, sizes, send, recv, peer, skip=0):
        si, ti, ni = cut(step[0], at[0], sizes[0], widths[0], skip)
        sj, tj, nj = cut(step[1], at[1], sizes[1], widths[1], 0)
        return pltpu.make_async_remote_copy(
            src_ref=ref.at[(*lead, pl.ds(si, ni), pl.ds(sj, nj))],
            dst_ref=ref.at[(*lead, pl.ds(ti, ni), pl.ds(tj, nj))],
            send_sem=send, recv_sem=recv, device_id=peer, device_id_type=MESH,
        )

    def side_of(step):
        return side_sem.at[step[0] % 3]

    def stage_a(step, peer):
        def part(lead, width):
            return message(
                x0, (lead,), step, (width, width), (I0, J0), (W0, W0), send_sem.at[0], side_of(step), peer
            )

        return [] if step[0] and step[1] else [part(pl.ds(0, 2), 2), part(2, 3)]

    def send_corners(across):
        for ci, cj in CORNERS:
            for di, dj in ((0, 1), (1, 0), (1, 1)):
                if (di and dj) != across:
                    continue
                step = ((2 * ci - 1) * di, (2 * cj - 1) * dj)
                if di and dj:
                    parts = ((pl.ds(0, 2), (0, 4), (0, 4)), (2, (0, 5), (0, 5)))
                elif di:
                    parts = ((pl.ds(0, 2), (2, 2), (0, 3)), (2, (3, 2), (0, 3)))
                else:
                    parts = ((pl.ds(0, 2), (0, 3), (2, 2)), (2, (0, 3), (3, 2)))
                there = CORNERS.index((ci ^ di, cj ^ dj))
                ok, peer = reach(step)

                @pl.when(ok)
                def _():
                    for lead, (ri, ni), (rj, nj) in parts:
                        pi, pj = (5 - ri - ni if ci else ri), (5 - rj - nj if cj else rj)
                        pltpu.make_async_remote_copy(
                            src_ref=x0.at[lead, pl.ds(I0 + 11 * ci + pi, ni), pl.ds(J0 + 11 * cj + pj, nj)],
                            dst_ref=px.at[
                                there, lead, pl.ds(5 * (1 - ci) + pi, ni), pl.ds(K0 + 5 * (1 - cj) + pj, nj)
                            ],
                            send_sem=send_sem.at[4], recv_sem=recv_sem.at[3], device_id=peer, device_id_type=MESH,
                        ).start()

    def stage_b(step, peer):
        def part(lead, widths, skip=0):
            return message(
                x1, (lead,), step, widths, (I1, J1), (H1, W1), send_sem.at[1], recv_sem.at[0], peer, skip
            )

        if step[0] and step[1]:
            return [part(pl.ds(0, 2), (1, 6)), part(pl.ds(0, 2), (2, 4), 1)]
        return [part(0, (3, 0)), part(1, (4, 0))] if step[0] else [part(pl.ds(0, 2), (0, 7))]

    def stage_c(step, peer):
        def part(widths, skip=0):
            return message(f1, (), step, widths, (I1, J1), (H1, W1), send_sem.at[2], recv_sem.at[1], peer, skip)

        return [part((1, 5)), part((2, 3), 1)] if step[0] and step[1] else [part((3, 6))]

    size_a, size_b, size_c = (7 * W0, 7 * W0, 0), (56, 56, 28), (24, 24, 11)
    size_k = (2 * 18, 2 * 18, 57)

    def all_of(size):
        return lambda nb, ng: nb * size[0] + ng * size[1] + nb * ng * size[2]

    def each(stage):
        for step in DIRS:
            ok, peer = reach(step)

            @pl.when(ok)
            def _():
                for copy in stage(step, peer):
                    copy.start()

    tell(0)
    each(stage_a)
    send_corners(0)
    x1[(0, *own1)] = pack_pool(x0[(1, *own0)], pool0)
    x1[(1, *own1)] = pack_pool(x0[(2, *own0)], pool0)
    hear(0)
    tell(1)

    block = (x0, inv0, y0, cy0, x20, cx20, base0)

    def diagonal(at, n, fields=block, cols=J8):
        x, inv, y, cy, _, _, _ = fields
        rows = pl.ds(at, n)
        f, m, c = x[0, rows, cols], x[1, rows, cols], x[2, rows, cols]
        invd = inverse(m, c, around_at(x.at[2], at, n, cols))
        first = f * invd
        inv[rows, cols], y[rows, cols], cy[rows, cols] = invd, first, c * first

    def second(at, n, fields=block, cols=J8):
        x, inv, y, cy, x2, cx2, base = fields
        rows = pl.ds(at, n)
        f, c = x[0, rows, cols], x[2, rows, cols]
        s = (0.125 * beta) * (c * around_at(y, at, n, cols) + around_at(cy, at, n, cols))
        fix = inv[rows, cols] * (alpha * f + s)
        x2[rows, cols], cx2[rows, cols], base[rows, cols] = fix, c * fix, (1.0 - alpha) * f - s

    def residual(at, n, fields=block, cols=J8):
        x, _, _, _, x2, cx2, base = fields
        rows = pl.ds(at, n)
        total = x[2, rows, cols] * around_at(x2, at, n, cols) + around_at(cx2, at, n, cols)
        return base[rows, cols] + 0.125 * total

    drain_by_place(side_sem.at[0], lambda nb, ng: ng * size_a[1])
    send_corners(1)
    each(stage_b)
    diagonal(4, 14)
    second(5, 12)
    r0[6:16] = residual(6, 10)
    f1[pl.ds(I1 + 1, 2), pl.ds(J1, W1), :] = pack_pool(r0[7:15], pool0, J0 - 8)
    hear(1)
    tell(2)
    run = 4
    for turn_no in range(2):
        low = (lax.rem(b, run) != 0) if turn_no == 0 else (lax.rem(b, run) == 0)

        def arrived(nb, ng):
            return size_a[0]

        drain_by_place(side_sem.at[1], arrived, low & (b > 0))
        drain_by_place(side_sem.at[2], arrived, ~low & (b < bricks - 1))
        diagonal(jnp.where(low, 1, 18), 3)
        second(jnp.where(low, 2, 17), 3)
        r0[pl.ds(jnp.where(low, 3, 16), 3)] = residual(jnp.where(low, 3, 16), 3)
        quad = pack_pool(r0[pl.ds(jnp.where(low, 3, 15), 4)], pool0, J0 - 8)
        f1[pl.ds(jnp.where(low, I1, I1 + 3), 1), pl.ds(J1, W1), :] = quad
    each(stage_c)
    fine_ref[...] = x20[own0]

    drain_by_place(recv_sem.at[3], all_of(size_k))
    for v, (ci, cj) in enumerate(CORNERS):
        own_i, own_j = 5 * (1 - ci), K0 + 5 * (1 - cj)
        for lead, deep in ((pl.ds(0, 2), 2), (pl.ds(2, 1), 3)):
            for at_i, ni, at_j, nj in ((-deep * (1 - ci), 5 + deep, 0, 5), (0, 5, 5 if cj else -deep, deep)):
                px[v, lead, pl.ds(own_i + at_i, ni), pl.ds(own_j + at_j, nj), :] = x0[
                    lead, pl.ds(I0 + 11 * ci + at_i, ni), pl.ds(J0 + 11 * cj + at_j, nj), :
                ]
        patch = (px.at[v], *(work.at[v, i] for i in range(6)))
        diagonal(1, 8, patch, J4)
        second(2, 6, patch, J4)
        r2 = residual(3, 4, patch, J4)
        pair = halve(jnp.stack([r2[0] + r2[1], r2[2] + r2[3]]), pool3.at[v], 2, 2)
        near[v, 0] = 0.125 * (pair[0] + turn(pair[0], 1))
        near[v, 1] = 0.125 * (pair[1] + turn(pair[1], -1))
        fine_ref[pl.ds(15 * ci, 1), pl.ds(15 * cj, 1), :] = work[v, 3, pl.ds(5 - ci, 1), pl.ds(K0 + 5 - cj, 1), :]

    drain_by_place(recv_sem.at[0], all_of(size_b))
    m1, c1 = x1[0], x1[1]
    c2 = unpack_pool(c1, pool1)
    m2 = unpack_pool(m1, pool1)
    invd1[...] = inverse(m1[1:-1], c1[1:-1], weigh(c1, 2, pairs_beside, w1))
    invd2[...] = inverse(m2[1:-1], c2[1:-1], weigh(c2, 4, rows_beside, w2))
    drain_by_place(send_sem.at[0], all_of(size_a))
    drain_by_place(send_sem.at[1], all_of(size_b))

    drain_by_place(send_sem.at[4], all_of(size_k))
    drain_by_place(send_sem.at[2], all_of(size_c))
    drain_by_place(recv_sem.at[1], all_of(size_c))
    for v, (ci, cj) in enumerate(CORNERS):
        for lower in range(2):
            at = (I1 - 1 + H1 * ci + lower, pl.ds(J1 - 1 + W1 * cj, 2))
            old = f1[at]
            f1[at] = jnp.where(lanes_of(old) % 2 == 1 - lower, near[v, lower], old)
    f = f1[1:-1]
    invd = invd1[...]
    edge = jnp.zeros((1, *E1[1:]), jnp.float32)
    y = jnp.concatenate([edge, f * invd, edge], axis=0)
    s = beta * spread(y, 2, pairs_beside, lambda i: w1[i])
    x2 = invd * (alpha * f + s)
    middle = x2[3:7, J1 : J1 + W1]
    r2 = (1.0 - alpha) * f[1:-1] - s[1:-1] + spread(x2, 2, pairs_beside, lambda i: w1[i, 1:9])

    f = unpack_pool(r2, pool1)
    invd = invd2[1:9]
    s = beta * spread(f * invd, 4, rows_beside, lambda i: w2[i, 2:8])
    x2 = invd[1:-1] * (alpha * f[1:-1] + s)
    coarse = x2[1:5, 4:8]
    r2 = (1.0 - alpha) * f[2:-2] - s[1:-1] + spread(x2, 4, rows_beside, lambda i: w2[i, 3:7])

    pool2[0], pool2[1] = r2[0] + r2[1], r2[2] + r2[3]
    both = pool2[:, pl.ds(4, 2, stride=2), :] + pool2[:, pl.ds(5, 2, stride=2), :]
    upper = both[0] + turn(both[0], -4)
    lower = turn(both[1], 1) + turn(both[1], -3)
    f3[...] = 0.125 * jnp.where(lanes_of(upper) % 2 == 0, upper, lower)

    hear(2)
    for k in mates:
        pltpu.make_async_remote_copy(
            src_ref=f3, dst_ref=gather_ref.at[g], send_sem=send_sem.at[3], recv_sem=recv_sem.at[2],
            device_id=mate(k), device_id_type=MESH,
        ).start()

    gather_ref[g] = f3[...]
    flat = middle.reshape(H1 * W1, LANES)
    for side in range(2):
        rows = squeeze(flat, 2, side).reshape(H1, W1, LANES // 2)
        for i in range(H1):
            middle_ref[2 * i + side] = rows[i]
    for i in range(4):
        coarse_ref[i] = squeeze(coarse[i], 4)

    drain(send_sem.at[3], 2 * (groups - 1))
    drain(recv_sem.at[2], 2 * (groups - 1))


def finish_kernel(fine, middle, coarse, gathered, fine_out, middle_out, coarse_out, rhs_out, rhs, sem):
    copies = [
        pltpu.make_async_copy(source, target, sem.at[i])
        for i, (source, target) in enumerate(((fine, fine_out), (middle, middle_out), (coarse, coarse_out)))
    ]
    for copy in copies:
        copy.start()
    depth = rhs.shape[1]
    row = lax.broadcasted_iota(jnp.int32, (2 * depth, LANES), 0)
    lane = lax.broadcasted_iota(jnp.int32, (2 * depth, LANES), 1)
    pick = lane == 8 * (row % depth) + row // depth
    both = lax.dot_general(
        pick.astype(jnp.float32), gathered[...].reshape(-1, LANES), (((1,), (1,)), ((), ())),
        precision=lax.Precision.HIGHEST, preferred_element_type=jnp.float32,
    )
    rhs[0], rhs[1] = both[:depth], both[depth:]
    last = pltpu.make_async_copy(rhs, rhs_out, sem.at[3])
    last.start()
    for copy in (*copies, last):
        copy.wait()


def solution(mesh):
    bricks, groups = mesh.shape["brick"], mesh.shape["group"]
    anywhere = pl.BlockSpec(memory_space=pl.ANY)
    vmem = pl.BlockSpec(memory_space=pltpu.VMEM)

    def buf(*shape):
        return pltpu.VMEM(shape, jnp.float32)

    dma = pltpu.SemaphoreType.DMA

    def body(right_side, mass_coef, face_coef):
        small = ((W0, W0, LANES), (W1, W1, LANES // 2), (4, 4, LANES // 4))
        held = pl.pallas_call(
            functools.partial(main_kernel, bricks, groups),
            out_shape=(*(buf(*shape) for shape in small), buf(groups, 2, LANES)),
            in_specs=[anywhere] * 3,
            out_specs=(vmem,) * 4,
            scratch_shapes=[
                buf(3, *E0), buf(2, *E1), buf(*E1),
                *([buf(*E0)] * 6), buf(E0[0], 24, LANES),
                buf(2, 4, 24, LANES), buf(12, 24, LANES), buf(2, 12, LANES), buf(2, LANES),
                buf(3 * W0 * W0, LANES),
                buf(6, 10, 24, LANES), buf(6, 10, 12, LANES), buf(10, 24, LANES), buf(10, 12, LANES),
                buf(4, 3, *PATCH), buf(4, 6, *PATCH), buf(4, 2, 8, LANES), buf(4, 2, 2, LANES),
                dma, dma((5,)), dma((3,)), dma((4,)), pltpu.SemaphoreType.REGULAR((3,)),
            ],
            compiler_params=pltpu.CompilerParams(collective_id=0, has_side_effects=True),
            name="cycle",
        )(right_side, mass_coef, face_coef)
        held = [pltpu.with_memory_space_constraint(array, pltpu.VMEM) for array in held]
        rhs_shape = (2, LANES // 8, 2 * groups)
        fine, middle, coarse, rhs = pl.pallas_call(
            finish_kernel,
            out_shape=tuple(jax.ShapeDtypeStruct(shape, jnp.float32) for shape in (*small, rhs_shape)),
            in_specs=[vmem] * 4,
            out_specs=(anywhere,) * 4,
            scratch_shapes=[buf(*rhs_shape), dma((4,))],
            name="finish",
        )(*held)
        return fine, middle, coarse, jnp.swapaxes(rhs, 1, 2)

    placed = P("brick", "group", None)
    return jax.shard_map(
        body,
        mesh=mesh,
        in_specs=(placed, placed, placed),
        out_specs=(placed, placed, placed, P("brick", None, None)),
        check_vma=False,
    )
```
